32 devices in a mesh: dp: 16 (over z, y, core), tensor: 2 (over x).
Axes of the slice: x: 2, y: 2, z: 4, core: 2. Of those that a mesh axis runs over, the one named last changes fastest.
Arguments:
- hidden_rows: bfloat16 [1024, 16384], P('dp', 'tensor')
- norm_gain: float32 [16384], P('tensor'), may hold values from 0.5 to 1.5
- key_weight: bfloat16 [512, 16384], P('dp', 'tensor'), may hold values from -0.046875 to 0.046875
- cotangent: bfloat16 [16, 128, 512], P('dp'), may hold values from -6 to 6
- accepted_counts: int32 [16], P('dp'), may hold values from 16 to 64, as said below
- destination: int32 [1024], P('dp'), may hold values from 0 to 15, as said below
Outputs:
- keys: bfloat16 [16, 128, 512], P('dp')
- key_weight_grad: float32 [512, 16384], P('dp', 'tensor')
- gain_grad: float32 [16384], P('tensor')
The draws below stay inside these ranges and needn't reach their ends.
Inputs may be any that keep to these rules, and one draw needn't show every extreme that they name: `accepted_counts`: rows 0 to the count minus 1 of a replica are accepted; in every draw one replica accepts all its rows and another a quarter of them. `destination`: among one replica's 64 rows no shard is named more than 8 times; in every draw one shard is named exactly 8 times by every replica, all within the first quarter of that replica's rows.
All inputs are finite; a program needn't handle non-finite values.
Results may differ from the reference program's by a relative error of at most 0.0051.
Values may be sent and summed in bfloat16 or wider, within the bound.
No kernel may reach another device: no remote copies, remote signals or barrier semaphores. Data moves between devices by JAX's collectives and lax.ppermute only.
A program may use at most 64 MiB of HBM per device.

```python
import math
import jax
import jax.numpy as jnp
from jax import lax

D = 16384
KVW = 512
ROWS = 64
DATA_COPIES = 16
CAP = 8
SLOTS = 128
TOTAL_ROWS = 1024


def draw_hidden_rows(key, part):
    key_noise, key_row, key_column = jax.random.split(key, 3)
    position = jnp.arange(D, dtype=jnp.float32) / D
    noise_base = jnp.clip(jax.random.normal(key_noise, (TOTAL_ROWS, D), jnp.float32), -6.0, 6.0)
    rising = jnp.exp(position * (0.5 * math.log(4.0)))
    row_scale = jnp.exp(jax.random.uniform(key_row, (TOTAL_ROWS, 1), jnp.float32, 0.0, math.log(10.0)))
    column_scale = jnp.exp(jax.random.uniform(key_column, (D,), jnp.float32, 0.0, math.log(10.0)))
    return (noise_base * row_scale * (column_scale * rising)[None, :]).astype(jnp.bfloat16)


def draw_accepted_counts(key, part):
    key_values, key_top, key_low = jax.random.split(key, 3)
    counted = jax.random.randint(key_values, (DATA_COPIES,), ROWS // 4, ROWS + 1)
    top_replica = jax.random.randint(key_top, (), 0, DATA_COPIES)
    low_replica = (top_replica + 1 + jax.random.randint(key_low, (), 0, DATA_COPIES - 1)) % DATA_COPIES
    return counted.at[top_replica].set(ROWS).at[low_replica].set(ROWS // 4).astype(jnp.int32)


def draw_destination(key, part):
    busiest_key, extra_token_key, rows_key_seed = jax.random.split(key, 3)
    position_count = DATA_COPIES * CAP
    busiest_partition = jax.random.randint(busiest_key, (), 0, DATA_COPIES)
    partition_index = jnp.arange(DATA_COPIES, dtype=jnp.int32)
    extra_token = jax.random.randint(extra_token_key, (DATA_COPIES,), 0, 4)
    extra_token = jnp.where(partition_index == busiest_partition, 8, extra_token)
    position_index = jnp.arange(position_count, dtype=jnp.int32)
    position_holder = position_index // CAP
    row_ids = jnp.arange(ROWS, dtype=jnp.int32)

    def one_replica(replica):
        key_replica = jax.random.fold_in(rows_key_seed, replica)
        key_pick, key_rank, key_place = jax.random.split(key_replica, 3)
        random_selection = jax.random.randint(key_pick, (position_count,), 0, 16384)
        priority_rating = (extra_token[position_holder] * 16384 + random_selection) * position_count + position_index
        chosen = lax.top_k(priority_rating, ROWS)[1]
        target = chosen // CAP
        is_hot = target == busiest_partition
        rank_key = jnp.where(is_hot, 16384, jax.random.randint(key_rank, (ROWS,), 0, 16384)) * ROWS + row_ids
        ranking = jnp.argsort(jnp.argsort(rank_key))
        early = is_hot | (ranking < ROWS // 4 - CAP)
        place_key = jnp.where(early, 0, 16384) + jax.random.randint(key_place, (ROWS,), 0, 16384)
        place_key = place_key * ROWS + row_ids
        return target[jnp.argsort(place_key)]
    return jax.vmap(one_replica)(partition_index).reshape(-1).astype(jnp.int32)


def with_spikes(result, rng, source, target, parts, factor):
    def block_of(dim):
        return (jnp.arange(result.shape[dim]) // (result.shape[dim] // parts)).reshape((-1,) + (1,) * (result.ndim - 1 - dim))

    first = jax.random.permutation(rng, parts)[block_of(target)]
    second = (block_of(target) + parts // 2) % parts
    return jnp.where((block_of(source) == first) | (block_of(source) == second), factor * result, result)


def level_of(stream_key, dims, shards, least, top_value):
    def one(dim, parts):
        steps = jax.random.uniform(jax.random.fold_in(jax.random.fold_in(stream_key, 6), dim), (parts,), jnp.float32, least / len(shards), top_value / len(shards))
        return jnp.repeat(jnp.exp(steps), dims[dim] // parts).reshape((-1,) + (1,) * (len(dims) - dim - 1))

    factor_of = one(*shards[0])
    for cut in shards[1:]:
        factor_of = factor_of * one(*cut)
    return factor_of


def bell_draw(stream_key, extent, deviation, reach, cuts=(), held_as=jnp.bfloat16):
    gain = level_of(stream_key, extent, cuts, -0.22, 0.18) if cuts else 1.0
    array = jax.random.normal(stream_key, extent, jnp.float32) * deviation * gain
    return jnp.minimum(jnp.maximum(array, -reach), reach).astype(held_as)


def noise_with(stream_key, dims, scale, reach, cuts, heavy, held_as=jnp.bfloat16):
    entries = scale * jax.random.normal(stream_key, dims, jnp.float32)
    if cuts:
        entries = entries * level_of(stream_key, dims, cuts, -0.22, 0.18)
    return jnp.clip(with_spikes(entries, jax.random.fold_in(stream_key, 3), *heavy), -reach, reach).astype(held_as)


def setup_inputs(seed: int = 0) -> dict:
    splits = jax.random.split(jax.random.key(seed), 7)
    hidden_rows = draw_hidden_rows(jax.random.fold_in(splits[6], 71), 0)
    norm_gain = jnp.clip(1.0 + 0.1 * jax.random.normal(splits[1], (D,), jnp.float32), 0.5, 1.5)
    key_weight = bell_draw(splits[2], (KVW, D), D ** -0.5, 0.046875, ((0, 16), (1, 2)))
    cotangent = noise_with(splits[3], (DATA_COPIES, SLOTS, KVW), 1.0, 6.0, ((0, 16),), (0, 2, 16, 2.0))
    accepted_counts = draw_accepted_counts(jax.random.fold_in(splits[6], 71), 0)
    destination = draw_destination(jax.random.fold_in(splits[6], 71), 0)
    return dict(hidden_rows=hidden_rows, norm_gain=norm_gain, key_weight=key_weight, cotangent=cotangent, accepted_counts=accepted_counts, destination=destination)


EPSILON = 1e-05

def layout(dest_rows, count):
    row_total = dest_rows.shape[0]
    row_order = jnp.arange(row_total, dtype=jnp.int32)
    onehot = (dest_rows[:, None] == jnp.arange(DATA_COPIES, dtype=jnp.int32)[None, :]).astype(jnp.int32)
    before = jnp.cumsum(onehot, axis=0) - onehot
    slot_rank = lax.optimization_barrier(jnp.sum(before * onehot, axis=1)).astype(jnp.int32)
    return (row_order < count, slot_rank)

def reference(hidden_rows, norm_gain, key_weight, cotangent, accepted_counts, destination):
    factor = 1.0 / math.sqrt(TOTAL_ROWS)
    blocks = hidden_rows.reshape(DATA_COPIES, ROWS, D)
    targets = destination.reshape(DATA_COPIES, ROWS)

    def one_replica(running, inputs):
        grad_weight, grad_gain = running
        row_data, dest_rows, count, replica = inputs
        accepted, slot_rank = layout(dest_rows, count)
        row_values = jnp.where(accepted[:, None], row_data.astype(jnp.float32), jnp.float32(0.0))
        mean_square = lax.optimization_barrier(jnp.sum(row_values * row_values, axis=1)) / D
        normed = (row_values * lax.rsqrt(mean_square + EPSILON)[:, None] * norm_gain[None, :]).astype(jnp.bfloat16)
        row_keys = lax.dot_general(normed, key_weight, (((1,), (1,)), ((), ())), preferred_element_type=jnp.float32).astype(jnp.bfloat16)
        slot_column = (replica * CAP + slot_rank).astype(jnp.int32)
        row_cotangent = cotangent[dest_rows, slot_column]
        grad_weight = grad_weight + lax.dot_general(row_cotangent, normed, (((0,), (0,)), ((), ())), preferred_element_type=jnp.float32)
        backward = jnp.dot(row_cotangent, key_weight, preferred_element_type=jnp.float32)
        grad_gain = grad_gain + lax.optimization_barrier(jnp.sum(backward * normed.astype(jnp.float32), axis=0))
        return ((grad_weight, grad_gain), (row_keys, slot_column, accepted))
    start_state = (jnp.zeros((KVW, D), jnp.float32), jnp.zeros((D,), jnp.float32))
    replica_ids = jnp.arange(DATA_COPIES, dtype=jnp.int32)
    (grad_weight, grad_gain), (all_keys, columns, accepted_all) = lax.scan(one_replica, start_state, (blocks, targets, accepted_counts, replica_ids))
    target_shard = jnp.where(accepted_all, targets, DATA_COPIES).astype(jnp.int32)
    keys = jnp.zeros((DATA_COPIES, SLOTS, KVW), jnp.bfloat16)
    keys = keys.at[target_shard.reshape(-1), columns.reshape(-1)].set(all_keys.reshape(-1, KVW), mode='drop')
    return (keys, grad_weight * factor, grad_gain * factor / norm_gain)
```

```python
import math

import jax
import jax.numpy as jnp
from jax import lax
from jax.sharding import Mesh
from jax.sharding import PartitionSpec as P

EPSILON = 1e-05

DP = ("hi", "low")


def reduce_tensor(value):
    if lax.axis_size("tensor") == 2:
        return value + lax.ppermute(value, "tensor", [(0, 1), (1, 0)])
    return lax.psum(value, "tensor")


def slot_onehot(dest_rows, count, shards, capacity):
    rows = dest_rows.shape[0]
    order = lax.broadcasted_iota(jnp.int32, (rows, rows), 0)
    other = lax.broadcasted_iota(jnp.int32, (rows, rows), 1)
    same = (dest_rows[:, None] == dest_rows[None, :]) & (other < order)
    rank = jnp.sum(same.astype(jnp.int32), axis=1)
    accepted = lax.iota(jnp.int32, rows) < count
    position = jnp.where(accepted, dest_rows * capacity + rank, -1)
    slots = lax.broadcasted_iota(jnp.int32, (rows, shards * capacity), 1)
    return accepted, (position[:, None] == slots).astype(jnp.bfloat16)


def on_device(hidden_rows, norm_gain, key_weight, cotangent, accepted_counts, destination):
    halves, low = lax.axis_size("hi"), lax.axis_size("low")
    replicas = halves * low
    rows, width = hidden_rows.shape
    tensor = lax.axis_size("tensor")
    model_width = width * tensor
    owned, key_width = key_weight.shape[0], cotangent.shape[2]
    part = width // low
    slots = cotangent.shape[1]
    capacity = slots // replicas

    weight_parts = key_weight.reshape(owned, low, part).transpose(1, 0, 2)
    weight_parts = jnp.broadcast_to(weight_parts[None], (halves, low, owned, part))
    weights = lax.all_to_all(
        weight_parts.reshape(replicas, owned, part), DP, split_axis=0, concat_axis=0, tiled=True
    ).reshape(key_width, part)

    returned = lax.all_to_all(cotangent[0], DP, split_axis=0, concat_axis=0, tiled=True)
    accepted, onehot = slot_onehot(destination, accepted_counts[0], replicas, capacity)
    row_cot = jnp.dot(onehot, returned, preferred_element_type=jnp.float32).astype(jnp.bfloat16)

    row_float = hidden_rows.astype(jnp.float32)
    squares = reduce_tensor(jnp.sum(row_float * row_float, axis=1))
    scale = lax.rsqrt(squares / model_width + EPSILON)
    normed = jnp.where(
        accepted[:, None], row_float * scale[:, None] * norm_gain[None, :], jnp.float32(0.0)
    ).astype(jnp.bfloat16)

    sent = jnp.concatenate(
        [
            normed.reshape(rows, low, part).transpose(1, 0, 2),
            jnp.broadcast_to(row_cot[None], (low, rows, key_width)),
        ],
        axis=2,
    )
    got = lax.all_to_all(sent, "low", split_axis=0, concat_axis=0, tiled=True)
    half_normed = got[:, :, :part].reshape(low * rows, part)
    half_cot = got[:, :, part:].reshape(low * rows, key_width)

    grad_part = lax.dot_general(
        half_cot, half_normed, (((0,), (0,)), ((), ())), preferred_element_type=jnp.float32
    )
    key_part = lax.dot_general(
        half_normed, weights, (((1,), (1,)), ((), ())), preferred_element_type=jnp.float32
    )
    gain_part = jnp.sum(grad_part * weights.astype(jnp.float32), axis=0)

    factor = 1.0 / math.sqrt(rows * replicas)
    grad_terms = lax.all_to_all(
        grad_part.astype(jnp.bfloat16).reshape(replicas, owned, part),
        DP,
        split_axis=0,
        concat_axis=0,
        tiled=True,
    ).reshape(halves, low, owned, part)
    grad_weight = (
        jnp.sum(grad_terms.astype(jnp.float32), axis=0).transpose(1, 0, 2).reshape(owned, width)
        * factor
    )

    gain_terms = lax.all_to_all(
        jnp.broadcast_to(gain_part[None, None], (replicas, 1, part)),
        DP,
        split_axis=0,
        concat_axis=0,
        tiled=True,
    ).reshape(halves, width)
    grad_gain = jnp.sum(gain_terms, axis=0) * factor / norm_gain

    key_terms = lax.all_to_all(
        key_part.astype(jnp.bfloat16).reshape(low, rows, key_width),
        "low",
        split_axis=0,
        concat_axis=0,
        tiled=True,
    )
    row_keys = reduce_tensor(jnp.sum(key_terms.astype(jnp.float32), axis=0)).astype(jnp.bfloat16)
    key_slots = lax.dot_general(
        onehot, row_keys, (((0,), (0,)), ((), ())), preferred_element_type=jnp.float32
    ).astype(jnp.bfloat16)
    key_out = lax.all_to_all(key_slots, DP, split_axis=0, concat_axis=0, tiled=True)
    return (key_out[None], grad_weight, grad_gain)


def solution(mesh):
    replicas, tensor = mesh.shape["dp"], mesh.shape["tensor"]
    split = Mesh(mesh.devices.reshape(2, replicas // 2, tensor), ("hi", "low", "tensor"))
    return jax.shard_map(
        on_device,
        mesh=split,
        in_specs=(
            P(DP, "tensor"),
            P("tensor"),
            P(DP, "tensor"),
            P(DP, None, None),
            P(DP),
            P(DP),
        ),
        out_specs=(P(DP, None, None), P(DP, "tensor"), P("tensor")),
        check_vma=False,
    )
```

```python
import math

import jax
import jax.numpy as jnp
from jax import lax
from jax.sharding import Mesh
from jax.sharding import PartitionSpec as P

EPSILON = 1e-05

DP = ("hi", "lo", "core")
SWAP = [(0, 1), (1, 0)]
FEW = 4


def iota2(shape, dim):
    return lax.broadcasted_iota(jnp.int32, shape, dim)


def select(matrix, table):
    return jnp.dot(matrix, table, preferred_element_type=jnp.float32).astype(jnp.bfloat16)


def reduce_tensor(value):
    if lax.axis_size("tensor") == 2:
        return value + lax.ppermute(value, "tensor", SWAP)
    return lax.psum(value, "tensor")


def peer(step):
    if lax.axis_size("lo") <= FEW:
        return lax.axis_index("lo") ^ step
    return step


def swap_lo(block):
    size = lax.axis_size("lo")
    if size > FEW:
        sent = jnp.stack([block(j) for j in range(size)])
        return lax.all_to_all(sent, "lo", split_axis=0, concat_axis=0, tiled=True)
    me = lax.axis_index("lo")
    got = [block(me)]
    for step in range(1, size):
        pairs = [(j, j ^ step) for j in range(size)]
        got.append(lax.ppermute(block(me ^ step), "lo", pairs))
    return jnp.stack(got)


def slot_onehot(dest_rows, count, shards, capacity):
    rows = dest_rows.shape[0]
    same = (dest_rows[:, None] == dest_rows[None, :]) & (
        iota2((rows, rows), 1) < iota2((rows, rows), 0)
    )
    rank = jnp.sum(same.astype(jnp.int32), axis=1)
    accepted = lax.iota(jnp.int32, rows) < count
    position = jnp.where(accepted, dest_rows * capacity + rank, -1)
    slots = iota2((rows, shards * capacity), 1)
    return accepted, (position[:, None] == slots).astype(jnp.bfloat16)


def on_device(hidden_rows, norm_gain, key_weight, cotangent, accepted_counts, destination):
    halves, low, cores = lax.axis_size("hi"), lax.axis_size("lo"), lax.axis_size("core")
    hi, core = lax.axis_index("hi"), lax.axis_index("core")
    replicas = halves * low * cores
    rows, width = hidden_rows.shape
    model_width = width * lax.axis_size("tensor")
    owned, key_width = key_weight.shape[0], cotangent.shape[2]
    part = width // low
    core_keys = key_width // cores
    capacity = cotangent.shape[1] // replicas

    weight_here = swap_lo(lambda j: lax.dynamic_slice(key_weight, (0, j * part), (owned, part)))
    weight_there = lax.ppermute(weight_here, "hi", SWAP)
    stacked = jnp.concatenate([weight_here, weight_there]).reshape(core_keys, part)
    square = (core_keys, core_keys)
    to, of = iota2(square, 0), iota2(square, 1)
    half_keys = low * owned
    same = (to // half_keys) == (hi ^ (of // half_keys))
    same &= (to % half_keys) // owned == peer((of % half_keys) // owned)
    same &= to % owned == of % owned
    weights = select(same.astype(jnp.bfloat16), stacked)

    returned = lax.all_to_all(cotangent[0], DP, split_axis=0, concat_axis=0, tiled=True)
    accepted, onehot = slot_onehot(destination, accepted_counts[0], replicas, capacity)
    row_cot = select(onehot, returned)

    row_float = hidden_rows.astype(jnp.float32)
    squares = reduce_tensor(jnp.sum(row_float * row_float, axis=1))
    scale = lax.rsqrt(squares / model_width + EPSILON)
    normed = jnp.where(
        accepted[:, None], row_float * scale[:, None] * norm_gain[None, :], jnp.float32(0.0)
    ).astype(jnp.bfloat16)

    sent = jnp.concatenate(
        [
            normed.reshape(rows, low, part).transpose(1, 0, 2),
            jnp.broadcast_to(row_cot[None], (low, rows, key_width)),
        ],
        axis=2,
    )
    got = lax.all_to_all(sent, "lo", split_axis=0, concat_axis=0, tiled=True)
    rows_here = got[:, :, :part].reshape(low * rows, part)
    rows_there = lax.ppermute(rows_here, "core", SWAP)
    square = (key_width, key_width)
    nat, col = iota2(square, 0), iota2(square, 1)
    from_col = (
        ((col % core_keys) // owned) * cores + (core ^ (col // core_keys))
    ) * owned + col % owned
    by_core = (nat == from_col).astype(jnp.bfloat16)
    cot_sorted = select(got[:, :, part:].reshape(low * rows, key_width), by_core)
    cot_here = cot_sorted[:, :core_keys]
    cot_there = lax.ppermute(cot_sorted[:, core_keys:], "core", SWAP)

    def grad_of(cot, normed_rows):
        return lax.dot_general(
            cot, normed_rows, (((0,), (0,)), ((), ())), preferred_element_type=jnp.float32
        )

    grad_part = grad_of(cot_here, rows_here) + grad_of(cot_there, rows_there)
    gain_part = jnp.sum(grad_part * weights.astype(jnp.float32), axis=0)

    factor = 1.0 / math.sqrt(rows * replicas)
    grad_terms = lax.all_to_all(
        grad_part.astype(jnp.bfloat16).reshape(halves * low, owned, part),
        ("hi", "lo"),
        split_axis=0,
        concat_axis=0,
        tiled=True,
    ).reshape(halves, low, owned, part)
    grad_weight = (
        jnp.sum(grad_terms.astype(jnp.float32), axis=0).transpose(1, 0, 2).reshape(owned, width)
        * factor
    )

    gain_terms = lax.all_to_all(
        jnp.broadcast_to(gain_part[None, None], (replicas, 1, part)),
        DP,
        split_axis=0,
        concat_axis=0,
        tiled=True,
    ).reshape(halves, low, cores, part)
    grad_gain = jnp.sum(gain_terms, axis=(0, 2)).reshape(width) * factor / norm_gain

    def keys_of(normed_rows):
        return lax.dot_general(
            normed_rows, weights, (((1,), (1,)), ((), ())), preferred_element_type=jnp.float32
        ).astype(jnp.bfloat16).reshape(low, 1, rows, core_keys)

    key_part = jnp.concatenate([keys_of(rows_here), keys_of(rows_there)], axis=1)
    key_terms = swap_lo(lambda j: lax.dynamic_index_in_dim(key_part, j, 0, keepdims=False))
    chip_keys = reduce_tensor(jnp.sum(key_terms.astype(jnp.float32), axis=0)).astype(jnp.bfloat16)
    row_keys = jnp.concatenate(
        [chip_keys[0], lax.ppermute(chip_keys[1], "core", SWAP)], axis=1
    )
    key_slots = lax.dot_general(
        onehot, row_keys, (((0,), (0,)), ((), ())), preferred_element_type=jnp.float32
    ).astype(jnp.bfloat16)
    key_slots = lax.dot_general(
        key_slots, by_core, (((1,), (1,)), ((), ())), preferred_element_type=jnp.float32
    ).astype(jnp.bfloat16)
    key_out = lax.all_to_all(key_slots, DP, split_axis=0, concat_axis=0, tiled=True)
    return (key_out[None], grad_weight, grad_gain)


def solution(mesh):
    replicas, tensor = mesh.shape["dp"], mesh.shape["tensor"]
    split = Mesh(
        mesh.devices.reshape(2, replicas // 4, 2, tensor), ("hi", "lo", "core", "tensor")
    )
    return jax.shard_map(
        on_device,
        mesh=split,
        in_specs=(
            P(DP, "tensor"),
            P("tensor"),
            P(DP, "tensor"),
            P(DP, None, None),
            P(DP),
            P(DP),
        ),
        out_specs=(P(DP, None, None), P(DP, "tensor"), P("tensor")),
        check_vma=False,
    )
```

```python
import functools
import math

import jax
import jax.numpy as jnp
from jax import lax
from jax.experimental import pallas as pl
from jax.experimental.pallas import tpu as pltpu
from jax.sharding import Mesh
from jax.sharding import PartitionSpec as P

EPSILON = 1e-05

DP = ("hi", "lo", "core")
SWAP = [(0, 1), (1, 0)]
FEW = 4
CHUNK = 512


def iota2(shape, dim):
    return lax.broadcasted_iota(jnp.int32, shape, dim)


def one_hot(index, size):
    return (index[:, None] == iota2((index.shape[0], size), 1)).astype(jnp.bfloat16)


def select(matrix, table):
    return jnp.dot(matrix, table, preferred_element_type=jnp.float32).astype(jnp.bfloat16)


def reduce_tensor(value):
    if lax.axis_size("tensor") == 2:
        return value + lax.ppermute(value, "tensor", SWAP)
    return lax.psum(value, "tensor")


def swap_core(value):
    return lax.ppermute(value, "core", SWAP)


def swap_lo(block):
    size, me = lax.axis_size("lo"), lax.axis_index("lo")
    if size <= FEW:
        pieces = [block(me)]
        for step in range(1, size):
            pairs = [(j, j ^ step) for j in range(size)]
            pieces.append(lax.ppermute(block(me ^ step), "lo", pairs))
        return pieces, [me ^ step for step in range(size)]
    sent = jnp.stack([block(j) for j in range(size)])
    got = lax.all_to_all(sent, "lo", split_axis=0, concat_axis=0, tiled=True)
    return [got.reshape((-1,) + got.shape[2:])], [jnp.int32(0)]


def slot_onehot(dest_rows, count, shards, capacity):
    rows = dest_rows.shape[0]
    same = (dest_rows[:, None] == dest_rows[None, :]) & (
        iota2((rows, rows), 1) < iota2((rows, rows), 0)
    )
    rank = jnp.sum(same.astype(jnp.int32), axis=1)
    accepted = lax.iota(jnp.int32, rows) < count
    position = jnp.where(accepted, dest_rows * capacity + rank, -1)
    return accepted, one_hot(position, shards * capacity)


def products_kernel(pieces, owned, low, core_keys, part, chunk, place_ref, *refs):
    row_refs, weight_refs = refs[: 2 * pieces], refs[2 * pieces : 2 * pieces + 2]
    own_ref, away_ref, gain_ref = refs[2 * pieces + 2 : 2 * pieces + 5]
    key_refs = refs[2 * pieces + 5 : 3 * pieces + 5]
    rows_ref, weights_ref, cot_ref, sums_ref, row_sem, weight_sem = refs[3 * pieces + 5 :]
    piece_rows = row_refs[0].shape[0]
    half_keys = core_keys // 2
    key_width = 2 * core_keys

    row_copies = [
        pltpu.make_async_copy(
            ref, rows_ref.at[pl.ds(j * piece_rows, piece_rows)], row_sem.at[j]
        )
        for j, ref in enumerate(row_refs)
    ]
    weight_copies = []
    block = half_keys // pieces
    for j in range(2 * pieces):
        first = place_ref[2 + j % pieces] * owned + (j // pieces) * half_keys
        if owned % 16 == 0:
            first = pl.multiple_of(first, 16)
        weight_copies.append(
            pltpu.make_async_copy(
                weight_refs[j // pieces].at[pl.ds((j % pieces) * block, block)],
                weights_ref.at[pl.ds(first, block)],
                weight_sem.at[j],
            )
        )
    for copy in row_copies + weight_copies:
        copy.start()
    for copy in row_copies:
        copy.wait()

    column = iota2((key_width, core_keys), 1)
    half = place_ref[0] ^ (column // half_keys)
    whole = ((half * low + (column % half_keys) // owned) * 2 + place_ref[1]) * owned
    whole = whole + column % owned
    chosen = jnp.where(iota2((key_width, core_keys), 0) == whole, 1.0, 0.0).astype(jnp.bfloat16)
    cot_ref[...] = lax.dot_general(
        rows_ref[:, part:], chosen, (((1,), (0,)), ((), ())), preferred_element_type=jnp.float32
    ).astype(jnp.bfloat16)
    for copy in weight_copies:
        copy.wait()

    for c in range(part // chunk):
        at = pl.ds(c * chunk, chunk)
        rows = rows_ref[:, at]
        weights = weights_ref[:, at]
        grad = lax.dot_general(
            cot_ref[...], rows, (((0,), (0,)), ((), ())), preferred_element_type=jnp.float32
        )
        own_ref[:, at] = grad[:half_keys]
        away_ref[:, at] = grad[half_keys:].astype(jnp.bfloat16)
        gain_ref[:, at] = jnp.sum(grad * weights.astype(jnp.float32), axis=0, keepdims=True)
        term = lax.dot_general(
            rows, weights, (((1,), (1,)), ((), ())), preferred_element_type=jnp.float32
        )
        if c == 0:
            sums_ref[...] = term
        else:
            sums_ref[...] += term
    for j, ref in enumerate(key_refs):
        for k in range(2):
            first = (k * pieces + j) * piece_rows
            ref[k] = sums_ref[first : first + piece_rows].astype(jnp.bfloat16)


def products(rows_here, rows_there, weights, places, core_keys, part, owned):
    pieces, low = len(rows_here), lax.axis_size("lo")
    piece_rows, columns = rows_here[0].shape
    half_keys = core_keys // 2
    scalars = jnp.stack([lax.axis_index("hi"), lax.axis_index("core")] + places).astype(jnp.int32)
    total = 2 * pieces * piece_rows
    return pl.pallas_call(
        functools.partial(
            products_kernel, pieces, owned, low, core_keys, part, min(CHUNK, part)
        ),
        out_shape=[
            jax.ShapeDtypeStruct((half_keys, part), jnp.float32),
            jax.ShapeDtypeStruct((half_keys, part), jnp.bfloat16),
            jax.ShapeDtypeStruct((1, part), jnp.float32),
        ]
        + [jax.ShapeDtypeStruct((2, piece_rows, core_keys), jnp.bfloat16)] * pieces,
        in_specs=[pl.BlockSpec(memory_space=pltpu.SMEM)]
        + [pl.BlockSpec(memory_space=pl.ANY)] * (2 * pieces + 2),
        scratch_shapes=[
            pltpu.VMEM((total, columns), jnp.bfloat16),
            pltpu.VMEM((core_keys, part), jnp.bfloat16),
            pltpu.VMEM((total, core_keys), jnp.bfloat16),
            pltpu.VMEM((total, core_keys), jnp.float32),
            pltpu.SemaphoreType.DMA((2 * pieces,)),
            pltpu.SemaphoreType.DMA((2 * pieces,)),
        ],
        compiler_params=pltpu.CompilerParams(vmem_limit_bytes=60 * 1024 * 1024),
        cost_estimate=pl.CostEstimate(
            flops=4 * total * core_keys * part,
            bytes_accessed=2 * total * columns + 8 * core_keys * part,
            transcendentals=0,
        ),
    )(scalars, *rows_here, *rows_there, *weights)


def on_device(hidden_rows, norm_gain, key_weight, cotangent, accepted_counts, destination):
    halves, low, cores = lax.axis_size("hi"), lax.axis_size("lo"), lax.axis_size("core")
    hi, core = lax.axis_index("hi"), lax.axis_index("core")
    replicas = halves * low * cores
    rows, width = hidden_rows.shape
    model_width = width * lax.axis_size("tensor")
    owned, key_width = key_weight.shape[0], cotangent.shape[2]
    part = width // low
    core_keys, half_keys = key_width // cores, low * owned
    capacity = cotangent.shape[1] // replicas
    factor = 1.0 / math.sqrt(rows * replicas)

    weight_here, places = swap_lo(
        lambda j: lax.dynamic_slice(key_weight, (0, j * part), (owned, part))
    )
    weight_here = jnp.concatenate(weight_here)
    weight_there = lax.ppermute(weight_here, "hi", SWAP)

    returned = lax.all_to_all(cotangent[0], DP, split_axis=0, concat_axis=0, tiled=True)
    accepted, onehot = slot_onehot(destination, accepted_counts[0], replicas, capacity)
    row_cot = select(onehot, returned)

    row_float = hidden_rows.astype(jnp.float32)
    squares = jnp.sum(row_float * row_float, axis=1)
    scale = lax.rsqrt(reduce_tensor(squares) / model_width + EPSILON)
    normed = jnp.where(
        accepted[:, None], row_float * scale[:, None] * norm_gain[None, :], jnp.float32(0.0)
    ).astype(jnp.bfloat16)

    rows_here, _ = swap_lo(
        lambda j: jnp.concatenate(
            [lax.dynamic_slice(normed, (0, j * part), (rows, part)), row_cot], axis=1
        )
    )
    rows_there = [swap_core(piece) for piece in rows_here]
    grad_own, grad_away, gain_part, *key_parts = products(
        rows_here, rows_there, (weight_here, weight_there), places, core_keys, part, owned
    )
    gain_part = gain_part[0]

    if low <= FEW:
        key_terms = [key_parts[0]] + [
            lax.ppermute(key_parts[step], "lo", [(j, j ^ step) for j in range(low)])
            for step in range(1, low)
        ]
    else:
        sent = key_parts[0].reshape(2, low, rows, core_keys).transpose(1, 0, 2, 3)
        got = lax.all_to_all(sent, "lo", split_axis=0, concat_axis=0, tiled=True)
        key_terms = [got[j] for j in range(low)]
    grad_away = lax.ppermute(grad_away, "hi", SWAP)
    key_sum = sum(term.astype(jnp.float32) for term in key_terms)
    chip_keys = reduce_tensor(key_sum).astype(jnp.bfloat16)
    row_keys = jnp.concatenate([chip_keys[0], swap_core(chip_keys[1])], axis=1)
    key_slots = lax.dot_general(
        onehot, row_keys, (((0,), (0,)), ((), ())), preferred_element_type=jnp.float32
    ).astype(jnp.bfloat16)
    place = lax.iota(jnp.int32, key_width)
    from_core = core ^ (place // core_keys)
    from_half = hi ^ ((place % core_keys) // half_keys)
    whole = ((from_half * low + (place % half_keys) // owned) * cores + from_core) * owned
    key_slots = select(key_slots, one_hot(whole + place % owned, key_width))
    upper = lax.reduce_precision(gain_part, 8, 7)
    terms = jnp.concatenate([upper, gain_part - upper]).astype(jnp.bfloat16)
    extra = -(-2 * part // (8 * key_width)) * 8
    terms = jnp.pad(terms, (0, extra * key_width - 2 * part)).reshape(1, extra, key_width)
    routed = jnp.concatenate(
        [
            key_slots.reshape(replicas, capacity, key_width),
            jnp.broadcast_to(terms, (replicas, extra, key_width)),
        ],
        axis=1,
    )

    grad_own, _ = lax.optimization_barrier((grad_own, routed))
    grad_own = ((grad_own + grad_away.astype(jnp.float32)) * factor).astype(jnp.bfloat16)
    grad_terms, _ = swap_lo(
        lambda j: lax.dynamic_slice(grad_own, (j * owned, 0), (owned, part))
    )
    if low <= FEW:
        grad_weight = jnp.zeros((owned, width), jnp.float32)
        for place, term in zip(places, grad_terms):
            grad_weight = lax.dynamic_update_slice(
                grad_weight, term.astype(jnp.float32), (0, place * part)
            )
    else:
        grad_weight = grad_terms[0].reshape(low, owned, part).transpose(1, 0, 2)
        grad_weight = grad_weight.reshape(owned, width).astype(jnp.float32)

    routed = lax.all_to_all(routed, DP, split_axis=0, concat_axis=0, tiled=True)
    key_out = routed[:, :capacity].reshape(1, replicas * capacity, key_width)
    gain_terms = routed[:, capacity:].reshape(replicas, extra * key_width)[:, : 2 * part]
    gain_sums = jnp.sum(
        gain_terms.astype(jnp.float32).reshape(halves, low, cores, 2, part), axis=(0, 2, 3)
    )
    grad_gain = gain_sums.reshape(width) * factor / norm_gain
    return (key_out, grad_weight, grad_gain)


def solution(mesh):
    replicas, tensor = mesh.shape["dp"], mesh.shape["tensor"]
    split = Mesh(
        mesh.devices.reshape(2, replicas // 4, 2, tensor), ("hi", "lo", "core", "tensor")
    )
    return jax.shard_map(
        on_device,
        mesh=split,
        in_specs=(
            P(DP, "tensor"),
            P("tensor"),
            P(DP, "tensor"),
            P(DP, None, None),
            P(DP),
            P(DP),
        ),
        out_specs=(P(DP, None, None), P(DP, "tensor"), P("tensor")),
        check_vma=False,
    )
```

```python
import functools
import math

import jax
import jax.numpy as jnp
from jax import lax
from jax.experimental import pallas as pl
from jax.experimental.pallas import tpu as pltpu
from jax.sharding import Mesh
from jax.sharding import PartitionSpec as P

EPSILON = 1e-05

DP = ("hi", "lo", "core")
SWAP = [(0, 1), (1, 0)]
FEW = 4
EARLY = 7
LANES = 128
CHUNK = 512


def iota2(shape, dim):
    return lax.broadcasted_iota(jnp.int32, shape, dim)


def one_hot(index, size):
    return (index[:, None] == iota2((index.shape[0], size), 1)).astype(jnp.bfloat16)


def select(matrix, table):
    return jnp.dot(matrix, table, preferred_element_type=jnp.float32).astype(jnp.bfloat16)


def reduce_tensor(value):
    if lax.axis_size("tensor") == 2:
        return value + lax.ppermute(value, "tensor", SWAP)
    return lax.psum(value, "tensor")


def swap_core(value):
    return lax.ppermute(value, "core", SWAP)


def swap_lo(block):
    size, me = lax.axis_size("lo"), lax.axis_index("lo")
    if size <= FEW:
        pieces = [block(me)]
        for step in range(1, size):
            pairs = [(j, j ^ step) for j in range(size)]
            pieces.append(lax.ppermute(block(me ^ step), "lo", pairs))
        return pieces, [me ^ step for step in range(size)]
    sent = jnp.stack([block(j) for j in range(size)])
    got = lax.all_to_all(sent, "lo", split_axis=0, concat_axis=0, tiled=True)
    return [got.reshape((-1,) + got.shape[2:])], [jnp.int32(0)]


def slot_onehot(dest_rows, count, shards, capacity):
    rows = dest_rows.shape[0]
    same = (dest_rows[:, None] == dest_rows[None, :]) & (
        iota2((rows, rows), 1) < iota2((rows, rows), 0)
    )
    rank = jnp.sum(same.astype(jnp.int32), axis=1)
    accepted = lax.iota(jnp.int32, rows) < count
    position = jnp.where(accepted, dest_rows * capacity + rank, -1)
    return accepted, one_hot(position, shards * capacity)


def products_kernel(pieces, owned, low, core_keys, part, chunk, place_ref, *refs):
    row_refs, weight_refs = refs[: 2 * pieces], refs[2 * pieces : 2 * pieces + 2]
    grad_ref, gain_ref = refs[2 * pieces + 2 : 2 * pieces + 4]
    key_refs = refs[2 * pieces + 4 : 3 * pieces + 4]
    rows_ref, cot_ref, weights_ref, sums_ref, row_sem, cot_sem, weight_sem = refs[
        3 * pieces + 4 :
    ]
    piece_rows = row_refs[0].shape[0]
    half_keys = core_keys // 2
    key_width = 2 * core_keys

    copies = []
    for j, ref in enumerate(row_refs):
        at = pl.ds(j * piece_rows, piece_rows)
        first = part + j // pieces * core_keys
        for source, to, sem in (
            (ref.at[:, pl.ds(0, part)], rows_ref, row_sem),
            (ref.at[:, pl.ds(first, core_keys)], cot_ref, cot_sem),
        ):
            copies.append(pltpu.make_async_copy(source, to.at[at], sem.at[j]))
    block = half_keys // pieces
    for j in range(2 * pieces):
        first = place_ref[2 + j % pieces] * owned + (place_ref[0] ^ (j // pieces)) * half_keys
        if owned % 16 == 0:
            first = pl.multiple_of(first, 16)
        copies.append(
            pltpu.make_async_copy(
                weight_refs[j // pieces].at[pl.ds((j % pieces) * block, block)],
                weights_ref.at[pl.ds(first, block)],
                weight_sem.at[j],
            )
        )
    for copy in copies:
        copy.start()
    for copy in copies:
        copy.wait()

    for c in range(part // chunk):
        at = pl.ds(c * chunk, chunk)
        rows = rows_ref[:, at]
        weights = weights_ref[:, at]
        grad = lax.dot_general(
            cot_ref[...], rows, (((0,), (0,)), ((), ())), preferred_element_type=jnp.float32
        )
        grad_ref[:, at] = grad.astype(jnp.bfloat16)
        gain_ref[:, at] = jnp.sum(grad * weights.astype(jnp.float32), axis=0, keepdims=True)
        term = lax.dot_general(
            rows, weights, (((1,), (1,)), ((), ())), preferred_element_type=jnp.float32
        )
        if c == 0:
            sums_ref[...] = term
        else:
            sums_ref[...] += term
    for j, ref in enumerate(key_refs):
        for k in range(2):
            first = (k * pieces + j) * piece_rows
            ref[k] = sums_ref[first : first + piece_rows].astype(jnp.bfloat16)


def products(rows_here, rows_there, weights, places, core_keys, part, owned):
    pieces, low = len(rows_here), lax.axis_size("lo")
    piece_rows, columns = rows_here[0].shape
    half_keys = core_keys // 2
    scalars = jnp.stack([lax.axis_index("hi"), lax.axis_index("core")] + places).astype(jnp.int32)
    total = 2 * pieces * piece_rows
    return pl.pallas_call(
        functools.partial(
            products_kernel, pieces, owned, low, core_keys, part, min(CHUNK, part)
        ),
        out_shape=[
            jax.ShapeDtypeStruct((core_keys, part), jnp.bfloat16),
            jax.ShapeDtypeStruct((1, part), jnp.float32),
        ]
        + [jax.ShapeDtypeStruct((2, piece_rows, core_keys), jnp.bfloat16)] * pieces,
        in_specs=[pl.BlockSpec(memory_space=pltpu.SMEM)]
        + [pl.BlockSpec(memory_space=pl.ANY)] * (2 * pieces + 2),
        scratch_shapes=[
            pltpu.VMEM((total, part), jnp.bfloat16),
            pltpu.VMEM((total, core_keys), jnp.bfloat16),
            pltpu.VMEM((core_keys, part), jnp.bfloat16),
            pltpu.VMEM((total, core_keys), jnp.float32),
            pltpu.SemaphoreType.DMA((2 * pieces,)),
            pltpu.SemaphoreType.DMA((2 * pieces,)),
            pltpu.SemaphoreType.DMA((2 * pieces,)),
        ],
        compiler_params=pltpu.CompilerParams(vmem_limit_bytes=60 * 1024 * 1024),
        cost_estimate=pl.CostEstimate(
            flops=4 * total * core_keys * part,
            bytes_accessed=2 * total * columns + 8 * core_keys * part,
            transcendentals=0,
        ),
    )(scalars, *rows_here, *rows_there, *weights)


def sum_kernel(factor, terms_ref, grad_ref):
    low, _, part = terms_ref.shape[1:]
    for j in range(low):
        total = terms_ref[0, j].astype(jnp.float32) + terms_ref[1, j].astype(jnp.float32)
        grad_ref[:, pl.ds(j * part, part)] = total * factor


def sum_terms(terms, factor):
    _, low, owned, part = terms.shape
    return pl.pallas_call(
        functools.partial(sum_kernel, factor),
        out_shape=jax.ShapeDtypeStruct((owned, low * part), jnp.float32),
        in_specs=[pl.BlockSpec(memory_space=pltpu.VMEM)],
        out_specs=pl.BlockSpec(memory_space=pltpu.VMEM),
        compiler_params=pltpu.CompilerParams(vmem_limit_bytes=32 * 1024 * 1024),
        cost_estimate=pl.CostEstimate(
            flops=2 * terms.size, bytes_accessed=4 * terms.size, transcendentals=0
        ),
    )(terms)


def gather_kernel(key_rows, factor, place_ref, *refs):
    pieces, norm_ref, key_ref, gain_ref = refs[:-3], refs[-3], refs[-2], refs[-1]
    low, columns = len(pieces) // 2, key_ref.shape[1]
    half_rows, wide = (pieces[0].shape[0] - key_rows) // 2, columns // LANES
    for step, piece in enumerate(pieces):
        at = pl.multiple_of((place_ref[0] ^ step) * key_rows, key_rows)
        key_ref[pl.ds(at, key_rows)] = piece[:key_rows]
    for step in range(low):
        total = jnp.zeros((half_rows, columns), jnp.float32)
        for piece in pieces[step::low]:
            terms = piece[key_rows:].astype(jnp.float32)
            total = total + terms[:half_rows] + terms[half_rows:]
        for i in range(half_rows):
            for j in range(wide):
                at = pl.ds(((place_ref[1] ^ step) * half_rows + i) * wide + j, 1)
                sums = total[i : i + 1, j * LANES : (j + 1) * LANES]
                gain_ref[at] = sums * factor / norm_ref[at]


def gather_pieces(pieces, norm_gain, chip, key_rows, factor):
    places = jnp.stack([chip, lax.axis_index("lo")]).astype(jnp.int32)
    key_width, width = pieces[0].shape[1], norm_gain.shape[0]
    return pl.pallas_call(
        functools.partial(gather_kernel, key_rows, factor),
        out_shape=[
            jax.ShapeDtypeStruct((len(pieces) * key_rows, key_width), jnp.bfloat16),
            jax.ShapeDtypeStruct((width // LANES, LANES), jnp.float32),
        ],
        in_specs=[pl.BlockSpec(memory_space=pltpu.SMEM)]
        + [pl.BlockSpec(memory_space=pltpu.VMEM)] * (len(pieces) + 1),
        out_specs=[pl.BlockSpec(memory_space=pltpu.VMEM)] * 2,
    )(places, *pieces, norm_gain.reshape(width // LANES, LANES))


def on_device(hidden_rows, norm_gain, key_weight, cotangent, accepted_counts, destination):
    halves, low, cores = lax.axis_size("hi"), lax.axis_size("lo"), lax.axis_size("core")
    hi, lo, core = (lax.axis_index(name) for name in DP)
    replicas = halves * low * cores
    rows, width = hidden_rows.shape
    model_width = width * lax.axis_size("tensor")
    owned, key_width = key_weight.shape[0], cotangent.shape[2]
    part = width // low
    core_keys, half_keys = key_width // cores, low * owned
    capacity = cotangent.shape[1] // replicas
    factor = 1.0 / math.sqrt(rows * replicas)

    weight_here, places = swap_lo(
        lambda j: lax.dynamic_slice(key_weight, (0, j * part), (owned, part))
    )
    weight_here = jnp.concatenate(weight_here)
    weight_there = lax.ppermute(weight_here, "hi", SWAP)

    returned = lax.all_to_all(cotangent[0], DP, split_axis=0, concat_axis=0, tiled=True)
    accepted, onehot = slot_onehot(destination, accepted_counts[0], replicas, capacity)
    place = lax.iota(jnp.int32, key_width)
    from_core = core ^ (place // core_keys)
    whole = ((place % core_keys) // owned * cores + from_core) * owned + place % owned
    by_core = one_hot(whole, key_width)
    row_cot = lax.dot_general(
        select(onehot, returned),
        by_core,
        (((1,), (1,)), ((), ())),
        preferred_element_type=jnp.float32,
    ).astype(jnp.bfloat16)

    row_float = hidden_rows.astype(jnp.float32)
    squares = jnp.sum(row_float * row_float, axis=1)
    scale = lax.rsqrt(reduce_tensor(squares) / model_width + EPSILON)
    normed = jnp.where(
        accepted[:, None], row_float * scale[:, None] * norm_gain[None, :], jnp.float32(0.0)
    ).astype(jnp.bfloat16)

    rows_here, _ = swap_lo(
        lambda j: jnp.concatenate(
            [lax.dynamic_slice(normed, (0, j * part), (rows, part)), row_cot], axis=1
        )
    )
    rows_there = [swap_core(piece) for piece in rows_here]
    grad_part, gain_part, *key_parts = products(
        rows_here, rows_there, (weight_here, weight_there), places, core_keys, part, owned
    )
    gain_part = gain_part[0]

    if low <= FEW:
        key_terms = [key_parts[0]] + [
            lax.ppermute(key_parts[step], "lo", [(j, j ^ step) for j in range(low)])
            for step in range(1, low)
        ]
    else:
        sent = key_parts[0].reshape(2, low, rows, core_keys).transpose(1, 0, 2, 3)
        got = lax.all_to_all(sent, "lo", split_axis=0, concat_axis=0, tiled=True)
        key_terms = [got[j] for j in range(low)]
    grad_terms = lax.all_to_all(
        grad_part.reshape(halves * low, owned, part),
        ("hi", "lo"),
        split_axis=0,
        concat_axis=0,
        tiled=True,
    ).reshape(halves, low, owned, part)
    key_sum = sum(term.astype(jnp.float32) for term in key_terms)
    chip_keys = reduce_tensor(key_sum).astype(jnp.bfloat16)
    row_keys = jnp.concatenate([chip_keys[0], swap_core(chip_keys[1])], axis=1)
    key_slots = lax.dot_general(
        onehot, row_keys, (((0,), (0,)), ((), ())), preferred_element_type=jnp.float32
    ).astype(jnp.bfloat16)
    key_slots = select(key_slots, by_core)

    key_slots = key_slots.reshape(halves * low, cores, capacity, key_width)
    mine = lax.dynamic_index_in_dim(key_slots, core, 1, keepdims=False)
    other = swap_core(lax.dynamic_index_in_dim(key_slots, 1 - core, 1, keepdims=False))
    mine, other = jnp.where(core == 0, mine, other), jnp.where(core == 0, other, mine)
    gain_part = gain_part + swap_core(gain_part)
    upper = lax.reduce_precision(gain_part, 8, 7)
    terms = jnp.concatenate([upper, gain_part - upper]).astype(jnp.bfloat16)
    extra = -(-2 * part // (8 * key_width)) * 8
    terms = jnp.pad(terms, (0, extra * key_width - 2 * part)).reshape(1, extra, key_width)
    routed = jnp.concatenate(
        [mine, other, jnp.broadcast_to(terms, (halves * low, extra, key_width))], axis=1
    )
    late, grad_terms = lax.optimization_barrier((routed, grad_terms))
    grad_weight = sum_terms(grad_terms, factor)
    if low <= FEW:
        pieces = [
            lax.ppermute(
                lax.dynamic_index_in_dim(
                    routed if step < EARLY else late, (hi * low + lo) ^ step, 0, keepdims=False
                ),
                ("hi", "lo"),
                [(j, j ^ step) for j in range(halves * low)],
            )
            for step in range(1, halves * low)
        ]
        own = lax.dynamic_index_in_dim(routed, hi * low + lo, 0, keepdims=False)
        key_out, grad_gain = gather_pieces(
            [own] + pieces, norm_gain, hi * low + lo, cores * capacity, factor
        )
        grad_gain = grad_gain.reshape(width)
    else:
        routed = lax.all_to_all(routed, ("hi", "lo"), split_axis=0, concat_axis=0, tiled=True)
        key_out = routed[:, : cores * capacity].reshape(replicas * capacity, key_width)
        gain_sums = routed[:, cores * capacity :].reshape(halves, low, extra * key_width)
        gain_sums = gain_sums[:, :, : 2 * part].astype(jnp.float32)
        gain_sums = jnp.sum(gain_sums.reshape(halves, low, 2, part), axis=(0, 2))
        grad_gain = gain_sums.reshape(width) * factor / norm_gain
    return (key_out[None], grad_weight, grad_gain)


def solution(mesh):
    replicas, tensor = mesh.shape["dp"], mesh.shape["tensor"]
    split = Mesh(
        mesh.devices.reshape(2, replicas // 4, 2, tensor), ("hi", "lo", "core", "tensor")
    )
    return jax.shard_map(
        on_device,
        mesh=split,
        in_specs=(
            P(DP, "tensor"),
            P("tensor"),
            P(DP, "tensor"),
            P(DP, None, None),
            P(DP),
            P(DP),
        ),
        out_specs=(P(DP, None, None), P(DP, "tensor"), P("tensor")),
        check_vma=False,
    )
```

```python
import functools
import math

import jax
import jax.numpy as jnp
from jax import lax
from jax.experimental import pallas as pl
from jax.experimental.pallas import tpu as pltpu
from jax.sharding import Mesh
from jax.sharding import PartitionSpec as P

EPSILON = 1e-05

DP = ("hi", "lo", "core")
SWAP = [(0, 1), (1, 0)]
FEW = 4
PIN = 1
LANES = 128
CHUNK = 512


def iota2(shape, dim):
    return lax.broadcasted_iota(jnp.int32, shape, dim)


def one_hot(index, size):
    return (index[:, None] == iota2((index.shape[0], size), 1)).astype(jnp.bfloat16)


def select(matrix, table):
    return jnp.dot(matrix, table, preferred_element_type=jnp.float32).astype(jnp.bfloat16)


def reduce_tensor(value):
    if lax.axis_size("tensor") == 2:
        return value + lax.ppermute(value, "tensor", SWAP)
    return lax.psum(value, "tensor")


def swap_core(value):
    return lax.ppermute(value, "core", SWAP)


def swap_lo(block):
    size, me = lax.axis_size("lo"), lax.axis_index("lo")
    if size <= FEW:
        pieces = [block(me)]
        for step in range(1, size):
            pairs = [(j, j ^ step) for j in range(size)]
            pieces.append(lax.ppermute(block(me ^ step), "lo", pairs))
        return pieces, [me ^ step for step in range(size)]
    sent = jnp.stack([block(j) for j in range(size)])
    got = lax.all_to_all(sent, "lo", split_axis=0, concat_axis=0, tiled=True)
    return [got.reshape((-1,) + got.shape[2:])], [jnp.int32(0)]


def slot_onehot(dest_rows, count, shards, capacity):
    rows = dest_rows.shape[0]
    same = (dest_rows[:, None] == dest_rows[None, :]) & (
        iota2((rows, rows), 1) < iota2((rows, rows), 0)
    )
    rank = jnp.sum(same.astype(jnp.int32), axis=1)
    accepted = lax.iota(jnp.int32, rows) < count
    position = jnp.where(accepted, dest_rows * capacity + rank, -1)
    return accepted, one_hot(position, shards * capacity)


def products_kernel(pieces, owned, low, core_keys, part, chunk, *refs):
    row_refs, weight_refs = refs[: 2 * pieces], refs[2 * pieces : 2 * pieces + 2]
    grad_ref, gain_ref = refs[2 * pieces + 2 : 2 * pieces + 4]
    key_refs = refs[2 * pieces + 4 : 3 * pieces + 4]
    rows_ref, cot_ref, weights_ref, sums_ref, row_sem, cot_sem, weight_sem = refs[
        3 * pieces + 4 :
    ]
    piece_rows = row_refs[0].shape[0]
    half_keys = core_keys // 2
    key_width = 2 * core_keys

    copies = []
    for j, ref in enumerate(row_refs):
        at = pl.ds(j * piece_rows, piece_rows)
        first = part + j // pieces * core_keys
        for source, to, sem in (
            (ref.at[:, pl.ds(0, part)], rows_ref, row_sem),
            (ref.at[:, pl.ds(first, core_keys)], cot_ref, cot_sem),
        ):
            copies.append(pltpu.make_async_copy(source, to.at[at], sem.at[j]))
    block = half_keys // pieces
    for j in range(2 * pieces):
        place = lax.axis_index("lo") ^ j % pieces if pieces > 1 else 0
        first = place * owned + (lax.axis_index("hi") ^ (j // pieces)) * half_keys
        if owned % 16 == 0:
            first = pl.multiple_of(first, 16)
        copies.append(
            pltpu.make_async_copy(
                weight_refs[j // pieces].at[pl.ds((j % pieces) * block, block)],
                weights_ref.at[pl.ds(first, block)],
                weight_sem.at[j],
            )
        )
    for copy in copies:
        copy.start()
    for copy in copies:
        copy.wait()

    for c in range(part // chunk):
        at = pl.ds(c * chunk, chunk)
        rows = rows_ref[:, at]
        weights = weights_ref[:, at]
        grad = lax.dot_general(
            cot_ref[...], rows, (((0,), (0,)), ((), ())), preferred_element_type=jnp.float32
        )
        grad_ref[:, at] = grad.astype(jnp.bfloat16)
        gain_ref[:, at] = jnp.sum(grad * weights.astype(jnp.float32), axis=0, keepdims=True)
        term = lax.dot_general(
            rows, weights, (((1,), (1,)), ((), ())), preferred_element_type=jnp.float32
        )
        if c == 0:
            sums_ref[...] = term
        else:
            sums_ref[...] += term
    for j, ref in enumerate(key_refs):
        for k in range(2):
            first = (k * pieces + j) * piece_rows
            ref[k] = sums_ref[first : first + piece_rows].astype(jnp.bfloat16)


def products(rows_here, rows_there, weights, places, core_keys, part, owned):
    pieces, low = len(rows_here), lax.axis_size("lo")
    piece_rows, columns = rows_here[0].shape
    half_keys = core_keys // 2
    total = 2 * pieces * piece_rows
    return pl.pallas_call(
        functools.partial(
            products_kernel, pieces, owned, low, core_keys, part, min(CHUNK, part)
        ),
        out_shape=[
            jax.ShapeDtypeStruct((core_keys, part), jnp.bfloat16),
            jax.ShapeDtypeStruct((1, part), jnp.float32),
        ]
        + [jax.ShapeDtypeStruct((2, piece_rows, core_keys), jnp.bfloat16)] * pieces,
        in_specs=[pl.BlockSpec(memory_space=pl.ANY)] * (2 * pieces + 2),
        scratch_shapes=[
            pltpu.VMEM((total, part), jnp.bfloat16),
            pltpu.VMEM((total, core_keys), jnp.bfloat16),
            pltpu.VMEM((core_keys, part), jnp.bfloat16),
            pltpu.VMEM((total, core_keys), jnp.float32),
            pltpu.SemaphoreType.DMA((2 * pieces,)),
            pltpu.SemaphoreType.DMA((2 * pieces,)),
            pltpu.SemaphoreType.DMA((2 * pieces,)),
        ],
        compiler_params=pltpu.CompilerParams(vmem_limit_bytes=16 * 1024 * 1024),
        cost_estimate=pl.CostEstimate(
            flops=4 * total * core_keys * part,
            bytes_accessed=2 * total * columns + 8 * core_keys * part,
            transcendentals=0,
        ),
    )(*rows_here, *rows_there, *weights)


def sum_kernel(factor, terms_ref, grad_ref):
    low, _, part = terms_ref.shape[1:]
    for j in range(low):
        total = terms_ref[0, j].astype(jnp.float32) + terms_ref[1, j].astype(jnp.float32)
        grad_ref[:, pl.ds(j * part, part)] = total * factor


def sum_terms(terms, factor):
    _, low, owned, part = terms.shape
    return pl.pallas_call(
        functools.partial(sum_kernel, factor),
        out_shape=jax.ShapeDtypeStruct((owned, low * part), jnp.float32),
        in_specs=[pl.BlockSpec(memory_space=pltpu.VMEM)],
        out_specs=pl.BlockSpec(memory_space=pltpu.VMEM),
        compiler_params=pltpu.CompilerParams(vmem_limit_bytes=8 * 1024 * 1024),
        cost_estimate=pl.CostEstimate(
            flops=2 * terms.size, bytes_accessed=4 * terms.size, transcendentals=0
        ),
    )(terms)


def gather_kernel(key_rows, factor, *refs):
    pieces, norm_ref, key_ref, gain_ref = refs[:-3], refs[-3], refs[-2], refs[-1]
    low, columns = len(pieces) // 2, key_ref.shape[1]
    half_rows, wide = (pieces[0].shape[0] - 2 * key_rows) // 2, columns // LANES
    hi, lo, core = (lax.axis_index(name) for name in DP)
    mine = pl.ds(pl.multiple_of(core * key_rows, key_rows), key_rows)
    for step in range(low):
        place = lo ^ step
        total = jnp.zeros((half_rows, columns), jnp.float32)
        for k in range(2):
            piece = pieces[k * low + step]
            at = ((hi ^ core ^ k) * low + place) * key_rows
            key_ref[pl.ds(pl.multiple_of(at, key_rows), key_rows)] = piece[mine]
            terms = piece[2 * key_rows :].astype(jnp.float32)
            total = total + terms[:half_rows] + terms[half_rows:]
        for i in range(half_rows):
            for j in range(wide):
                at = pl.ds((place * half_rows + i) * wide + j, 1)
                sums = total[i : i + 1, j * LANES : (j + 1) * LANES]
                gain_ref[at] = sums * factor / norm_ref[at]


def gather_pieces(pieces, norm_gain, key_rows, factor):
    key_width, width = pieces[0].shape[1], norm_gain.shape[0]
    return pl.pallas_call(
        functools.partial(gather_kernel, key_rows, factor),
        out_shape=[
            jax.ShapeDtypeStruct((len(pieces) * key_rows, key_width), jnp.bfloat16),
            jax.ShapeDtypeStruct((width // LANES, LANES), jnp.float32),
        ],
        in_specs=[pl.BlockSpec(memory_space=pltpu.VMEM)] * (len(pieces) + 1),
        out_specs=[pl.BlockSpec(memory_space=pltpu.VMEM)] * 2,
        compiler_params=pltpu.CompilerParams(vmem_limit_bytes=4 * 1024 * 1024),
    )(*pieces, norm_gain.reshape(width // LANES, LANES))


def on_device(hidden_rows, norm_gain, key_weight, cotangent, accepted_counts, destination):
    halves, low, cores = lax.axis_size("hi"), lax.axis_size("lo"), lax.axis_size("core")
    hi, lo, core = (lax.axis_index(name) for name in DP)
    replicas = halves * low * cores
    rows, width = hidden_rows.shape
    model_width = width * lax.axis_size("tensor")
    owned, key_width = key_weight.shape[0], cotangent.shape[2]
    part = width // low
    core_keys, half_keys = key_width // cores, low * owned
    capacity = cotangent.shape[1] // replicas
    factor = 1.0 / math.sqrt(rows * replicas)

    weight_here, places = swap_lo(
        lambda j: lax.dynamic_slice(key_weight, (0, j * part), (owned, part))
    )
    weight_here = jnp.concatenate(weight_here)
    weight_there = lax.ppermute(weight_here, "hi", SWAP)

    returned = lax.all_to_all(cotangent[0], DP, split_axis=0, concat_axis=0, tiled=True)
    accepted, onehot = slot_onehot(destination, accepted_counts[0], replicas, capacity)
    place = lax.iota(jnp.int32, key_width)
    from_core = core ^ (place // core_keys)
    whole = ((place % core_keys) // owned * cores + from_core) * owned + place % owned
    by_core = one_hot(whole, key_width)
    row_cot = lax.dot_general(
        select(onehot, returned),
        by_core,
        (((1,), (1,)), ((), ())),
        preferred_element_type=jnp.float32,
    ).astype(jnp.bfloat16)

    row_float = hidden_rows.astype(jnp.float32)
    squares = jnp.sum(row_float * row_float, axis=1)
    scale = lax.rsqrt(reduce_tensor(squares) / model_width + EPSILON)
    normed = jnp.where(
        accepted[:, None], row_float * scale[:, None] * norm_gain[None, :], jnp.float32(0.0)
    ).astype(jnp.bfloat16)

    rows_here, _ = swap_lo(
        lambda j: jnp.concatenate(
            [lax.dynamic_slice(normed, (0, j * part), (rows, part)), row_cot], axis=1
        )
    )
    rows_there = [swap_core(piece) for piece in rows_here]
    grad_part, gain_part, *key_parts = products(
        rows_here, rows_there, (weight_here, weight_there), places, core_keys, part, owned
    )
    gain_part = gain_part[0]

    if low <= FEW:
        key_terms = [key_parts[0]] + [
            lax.ppermute(key_parts[step], "lo", [(j, j ^ step) for j in range(low)])
            for step in range(1, low)
        ]
    else:
        sent = key_parts[0].reshape(2, low, rows, core_keys).transpose(1, 0, 2, 3)
        got = lax.all_to_all(sent, "lo", split_axis=0, concat_axis=0, tiled=True)
        key_terms = [got[j] for j in range(low)]
    grad_terms = lax.all_to_all(
        grad_part.reshape(halves * low, owned, part),
        ("hi", "lo"),
        split_axis=0,
        concat_axis=0,
        tiled=True,
    ).reshape(halves, low, owned, part)
    key_sum = sum(term.astype(jnp.float32) for term in key_terms)
    chip_keys = reduce_tensor(key_sum).astype(jnp.bfloat16)
    row_keys = jnp.concatenate([chip_keys[0], swap_core(chip_keys[1])], axis=1)
    key_slots = lax.dot_general(
        onehot, row_keys, (((0,), (0,)), ((), ())), preferred_element_type=jnp.float32
    ).astype(jnp.bfloat16)
    key_slots = select(key_slots, by_core)

    whole_slots = key_slots.reshape(replicas, capacity, key_width)
    key_slots = key_slots.reshape(halves, low, cores, capacity, key_width)
    stay = lax.dynamic_index_in_dim(key_slots, hi ^ core, 0, keepdims=False)
    come = swap_core(lax.dynamic_index_in_dim(key_slots, hi ^ 1 ^ core, 0, keepdims=False))
    stay, come = jnp.where(core == 0, stay, come), jnp.where(core == 0, come, stay)
    gain_part = gain_part + swap_core(gain_part)
    upper = lax.reduce_precision(gain_part, 8, 7)
    terms = jnp.concatenate([upper, gain_part - upper]).astype(jnp.bfloat16)
    extra = -(-2 * part // (8 * key_width)) * 8
    terms = jnp.pad(terms, (0, extra * key_width - 2 * part)).reshape(1, extra, key_width)
    key_rows = cores * capacity
    routed = jnp.concatenate(
        [
            jnp.stack([stay, come], axis=2).reshape(low, cores * key_rows, key_width),
            jnp.broadcast_to(terms, (low, extra, key_width)),
        ],
        axis=1,
    )
    if low == FEW:
        pieces = [lax.dynamic_index_in_dim(routed, lo ^ s, 0, keepdims=False) for s in range(low)]
        own = pieces[0]
        pieces[PIN], grad_terms = lax.optimization_barrier((pieces[PIN], grad_terms))
        for step in range(low):
            pairs = [
                ((h * low + j) * cores + c, ((h ^ c) * low + (j ^ step)) * cores + c)
                for h in range(halves)
                for j in range(low)
                for c in range(cores)
                if step or c
            ]
            pieces[step] = lax.ppermute(pieces[step], DP, pairs)
        pieces[0] = jnp.where(core == 0, own, pieces[0])
        pieces += [swap_core(piece) for piece in pieces]
        key_out, grad_gain = gather_pieces(pieces, norm_gain, key_rows, factor)
        grad_gain = grad_gain.reshape(width)
    else:
        routed = lax.all_to_all(
            jnp.concatenate(
                [whole_slots, jnp.broadcast_to(terms, (replicas, extra, key_width))], axis=1
            ),
            DP, split_axis=0, concat_axis=0, tiled=True)
        key_out = routed[:, :capacity].reshape(replicas * capacity, key_width)
        gain_sums = routed[:, capacity:].reshape(replicas, extra * key_width)[:, : 2 * part]
        gain_sums = gain_sums.astype(jnp.float32).reshape(halves, low, cores, 2, part)
        gain_sums = jnp.sum(gain_sums[:, :, 0], axis=(0, 2))
        grad_gain = gain_sums.reshape(width) * factor / norm_gain
    return (key_out[None], sum_terms(grad_terms, factor), grad_gain)


def solution(mesh):
    replicas, tensor = mesh.shape["dp"], mesh.shape["tensor"]
    split = Mesh(
        mesh.devices.reshape(2, replicas // 4, 2, tensor), ("hi", "lo", "core", "tensor")
    )
    return jax.shard_map(
        on_device,
        mesh=split,
        in_specs=(
            P(DP, "tensor"),
            P("tensor"),
            P(DP, "tensor"),
            P(DP, None, None),
            P(DP),
            P(DP),
        ),
        out_specs=(P(DP, None, None), P(DP, "tensor"), P("tensor")),
        check_vma=False,
    )
```

```python
import functools
import math

import jax
import jax.numpy as jnp
from jax import lax
from jax.experimental import pallas as pl
from jax.experimental.pallas import tpu as pltpu
from jax.sharding import Mesh
from jax.sharding import PartitionSpec as P

EPSILON = 1e-05

DP = ("hi", "lo", "core")
SWAP = [(0, 1), (1, 0)]
FEW = 4
PIN = 1
LANES = 128
CHUNK = 512


def iota2(shape, dim):
    return lax.broadcasted_iota(jnp.int32, shape, dim)


def one_hot(index, size):
    return (index[:, None] == iota2((index.shape[0], size), 1)).astype(jnp.bfloat16)


def select(matrix, table):
    return jnp.dot(matrix, table, preferred_element_type=jnp.float32).astype(jnp.bfloat16)


def reduce_tensor(value):
    if lax.axis_size("tensor") == 2:
        return value + lax.ppermute(value, "tensor", SWAP)
    return lax.psum(value, "tensor")


def swap_core(value):
    return lax.ppermute(value, "core", SWAP)


def swap_lo(block):
    size, me = lax.axis_size("lo"), lax.axis_index("lo")
    if size <= FEW:
        pieces = [block(me)]
        for step in range(1, size):
            pairs = [(j, j ^ step) for j in range(size)]
            pieces.append(lax.ppermute(block(me ^ step), "lo", pairs))
        return pieces, [me ^ step for step in range(size)]
    sent = jnp.stack([block(j) for j in range(size)])
    got = lax.all_to_all(sent, "lo", split_axis=0, concat_axis=0, tiled=True)
    return [got.reshape((-1,) + got.shape[2:])], [jnp.int32(0)]


def slot_onehot(dest_rows, count, shards, capacity):
    rows = dest_rows.shape[0]
    same = (dest_rows[:, None] == dest_rows[None, :]) & (
        iota2((rows, rows), 1) < iota2((rows, rows), 0)
    )
    rank = jnp.sum(same.astype(jnp.int32), axis=1)
    accepted = lax.iota(jnp.int32, rows) < count
    position = jnp.where(accepted, dest_rows * capacity + rank, -1)
    return accepted, one_hot(position, shards * capacity)


def products_kernel(pieces, owned, core_keys, part, chunk, *refs):
    row_refs, weight_refs = refs[: 2 * pieces], refs[2 * pieces : 2 * pieces + 2]
    grad_ref, gain_ref = refs[2 * pieces + 2 : 2 * pieces + 4]
    key_refs = refs[2 * pieces + 4 : 3 * pieces + 4]
    rows_ref, cot_ref, weights_ref, sums_ref, row_sem, cot_sem, weight_sem = refs[
        3 * pieces + 4 :
    ]
    piece_rows = row_refs[0].shape[0]
    half_keys = core_keys // 2

    copies = []
    for j, ref in enumerate(row_refs):
        at = pl.ds(j * piece_rows, piece_rows)
        first = part + j // pieces * core_keys
        for source, to, sem in (
            (ref.at[:, pl.ds(0, part)], rows_ref, row_sem),
            (ref.at[:, pl.ds(first, core_keys)], cot_ref, cot_sem),
        ):
            copies.append(pltpu.make_async_copy(source, to.at[at], sem.at[j]))
    block = half_keys // pieces
    for j in range(2 * pieces):
        place = lax.axis_index("lo") ^ j % pieces if pieces > 1 else 0
        first = place * owned + (lax.axis_index("hi") ^ (j // pieces)) * half_keys
        if owned % 16 == 0:
            first = pl.multiple_of(first, 16)
        copies.append(
            pltpu.make_async_copy(
                weight_refs[j // pieces].at[pl.ds((j % pieces) * block, block)],
                weights_ref.at[pl.ds(first, block)],
                weight_sem.at[j],
            )
        )
    for copy in copies:
        copy.start()
    for copy in copies:
        copy.wait()

    for c in range(part // chunk):
        at = pl.ds(c * chunk, chunk)
        rows = rows_ref[:, at]
        weights = weights_ref[:, at]
        grad = lax.dot_general(
            cot_ref[...], rows, (((0,), (0,)), ((), ())), preferred_element_type=jnp.float32
        )
        grad_ref[:, at] = grad.astype(jnp.bfloat16)
        gain_ref[:, at] = jnp.sum(grad * weights.astype(jnp.float32), axis=0, keepdims=True)
        term = lax.dot_general(
            rows, weights, (((1,), (1,)), ((), ())), preferred_element_type=jnp.float32
        )
        if c == 0:
            sums_ref[...] = term
        else:
            sums_ref[...] += term
    for j, ref in enumerate(key_refs):
        for k in range(2):
            first = (k * pieces + j) * piece_rows
            ref[k] = sums_ref[first : first + piece_rows].astype(jnp.bfloat16)


def products(rows_here, rows_there, weights, core_keys, part, owned):
    pieces = len(rows_here)
    piece_rows, columns = rows_here[0].shape
    total = 2 * pieces * piece_rows
    return pl.pallas_call(
        functools.partial(
            products_kernel, pieces, owned, core_keys, part, min(CHUNK, part)
        ),
        out_shape=[
            jax.ShapeDtypeStruct((core_keys, part), jnp.bfloat16),
            jax.ShapeDtypeStruct((1, part), jnp.float32),
        ]
        + [jax.ShapeDtypeStruct((2, piece_rows, core_keys), jnp.bfloat16)] * pieces,
        in_specs=[pl.BlockSpec(memory_space=pl.ANY)] * (2 * pieces + 2),
        scratch_shapes=[
            pltpu.VMEM((total, part), jnp.bfloat16),
            pltpu.VMEM((total, core_keys), jnp.bfloat16),
            pltpu.VMEM((core_keys, part), jnp.bfloat16),
            pltpu.VMEM((total, core_keys), jnp.float32),
            pltpu.SemaphoreType.DMA((2 * pieces,)),
            pltpu.SemaphoreType.DMA((2 * pieces,)),
            pltpu.SemaphoreType.DMA((2 * pieces,)),
        ],
        compiler_params=pltpu.CompilerParams(vmem_limit_bytes=16 * 1024 * 1024),
        cost_estimate=pl.CostEstimate(
            flops=4 * total * core_keys * part,
            bytes_accessed=2 * total * columns + 8 * core_keys * part,
            transcendentals=0,
        ),
    )(*rows_here, *rows_there, *weights)


def sum_kernel(factor, terms_ref, grad_ref):
    low, _, part = terms_ref.shape[1:]
    for j in range(low):
        total = terms_ref[0, j].astype(jnp.float32) + terms_ref[1, j].astype(jnp.float32)
        grad_ref[:, pl.ds(j * part, part)] = total * factor


def sum_terms(terms, factor):
    _, low, owned, part = terms.shape
    return pl.pallas_call(
        functools.partial(sum_kernel, factor),
        out_shape=jax.ShapeDtypeStruct((owned, low * part), jnp.float32),
        in_specs=[pl.BlockSpec(memory_space=pltpu.VMEM)],
        out_specs=pl.BlockSpec(memory_space=pltpu.VMEM),
        compiler_params=pltpu.CompilerParams(vmem_limit_bytes=8 * 1024 * 1024),
        cost_estimate=pl.CostEstimate(
            flops=2 * terms.size, bytes_accessed=4 * terms.size, transcendentals=0
        ),
    )(terms)


def gather_kernel(key_rows, factor, *refs):
    pieces, norm_ref, key_ref, gain_ref = refs[:-3], refs[-3], refs[-2], refs[-1]
    low, columns = len(pieces) // 2, key_ref.shape[1]
    wide = columns // LANES
    half_rows = gain_ref.shape[0] // (low * wide)
    hi, lo, core = (lax.axis_index(name) for name in DP)
    mine = pl.ds(pl.multiple_of(core * key_rows, key_rows), key_rows)
    for step in range(low):
        place = lo ^ step
        total = jnp.zeros((half_rows, columns), jnp.float32)
        for k in range(2):
            piece = pieces[k * low + step]
            at = ((hi ^ core ^ k) * low + place) * key_rows
            key_ref[pl.ds(pl.multiple_of(at, key_rows), key_rows)] = piece[mine]
            terms = piece[2 * key_rows :].astype(jnp.float32)
            total = total + terms[:half_rows] + terms[half_rows : 2 * half_rows]
        for i in range(half_rows):
            for j in range(wide):
                at = pl.ds((place * half_rows + i) * wide + j, 1)
                sums = total[i : i + 1, j * LANES : (j + 1) * LANES]
                gain_ref[at] = sums * factor / norm_ref[at]


def gather_pieces(pieces, norm_gain, key_rows, factor):
    key_width, width = pieces[0].shape[1], norm_gain.shape[0]
    return pl.pallas_call(
        functools.partial(gather_kernel, key_rows, factor),
        out_shape=[
            jax.ShapeDtypeStruct((len(pieces) * key_rows, key_width), jnp.bfloat16),
            jax.ShapeDtypeStruct((width // LANES, LANES), jnp.float32),
        ],
        in_specs=[pl.BlockSpec(memory_space=pltpu.VMEM)] * (len(pieces) + 1),
        out_specs=[pl.BlockSpec(memory_space=pltpu.VMEM)] * 2,
        compiler_params=pltpu.CompilerParams(vmem_limit_bytes=4 * 1024 * 1024),
    )(*pieces, norm_gain.reshape(width // LANES, LANES))


def on_device(hidden_rows, norm_gain, key_weight, cotangent, accepted_counts, destination):
    halves, low, cores = lax.axis_size("hi"), lax.axis_size("lo"), lax.axis_size("core")
    hi, lo, core = (lax.axis_index(name) for name in DP)
    replicas = halves * low * cores
    rows, width = hidden_rows.shape
    model_width = width * lax.axis_size("tensor")
    owned, key_width = key_weight.shape[0], cotangent.shape[2]
    part = width // low
    core_keys = key_width // cores
    capacity = cotangent.shape[1] // replicas
    factor = 1.0 / math.sqrt(rows * replicas)

    weight_here, places = swap_lo(
        lambda j: lax.dynamic_slice(key_weight, (0, j * part), (owned, part))
    )
    weight_here = jnp.concatenate(weight_here)
    weight_there = lax.ppermute(weight_here, "hi", SWAP)

    returned = lax.all_to_all(cotangent[0], DP, split_axis=0, concat_axis=0, tiled=True)
    accepted, onehot = slot_onehot(destination, accepted_counts[0], replicas, capacity)
    place = lax.iota(jnp.int32, key_width)
    from_core = core ^ (place // core_keys)
    whole = ((place % core_keys) // owned * cores + from_core) * owned + place % owned
    by_core = one_hot(whole, key_width)
    row_cot = lax.dot_general(
        select(onehot, returned),
        by_core,
        (((1,), (1,)), ((), ())),
        preferred_element_type=jnp.float32,
    ).astype(jnp.bfloat16)

    row_float = hidden_rows.astype(jnp.float32)
    squares = jnp.sum(row_float * row_float, axis=1)
    scale = lax.rsqrt(reduce_tensor(squares) / model_width + EPSILON)
    normed = jnp.where(
        accepted[:, None], row_float * scale[:, None] * norm_gain[None, :], jnp.float32(0.0)
    ).astype(jnp.bfloat16)

    rows_here, _ = swap_lo(
        lambda j: jnp.concatenate(
            [lax.dynamic_slice(normed, (0, j * part), (rows, part)), row_cot], axis=1
        )
    )
    rows_there = [swap_core(piece) for piece in rows_here]
    grad_part, gain_part, *key_parts = products(
        rows_here, rows_there, (weight_here, weight_there), core_keys, part, owned
    )
    gain_part = gain_part[0]

    if low <= FEW:
        key_terms = [key_parts[0]] + [
            lax.ppermute(key_parts[step], "lo", [(j, j ^ step) for j in range(low)])
            for step in range(1, low)
        ]
    else:
        sent = key_parts[0].reshape(2, low, rows, core_keys).transpose(1, 0, 2, 3)
        got = lax.all_to_all(sent, "lo", split_axis=0, concat_axis=0, tiled=True)
        key_terms = [got[j] for j in range(low)]
    grad_terms = lax.all_to_all(
        grad_part.reshape(halves * low, owned, part),
        ("hi", "lo"),
        split_axis=0,
        concat_axis=0,
        tiled=True,
    ).reshape(halves, low, owned, part)
    key_sum = sum(term.astype(jnp.float32) for term in key_terms)
    chip_keys = reduce_tensor(key_sum).astype(jnp.bfloat16)
    row_keys = jnp.concatenate([chip_keys[0], swap_core(chip_keys[1])], axis=1)
    key_slots = lax.dot_general(
        onehot, row_keys, (((0,), (0,)), ((), ())), preferred_element_type=jnp.float32
    ).astype(jnp.bfloat16)
    key_slots = select(key_slots, by_core)

    whole_slots = key_slots.reshape(replicas, capacity, key_width)
    key_slots = key_slots.reshape(halves, low, cores, capacity, key_width)
    stay = lax.dynamic_index_in_dim(key_slots, hi ^ core, 0, keepdims=False)
    come = swap_core(lax.dynamic_index_in_dim(key_slots, hi ^ 1 ^ core, 0, keepdims=False))
    stay, come = jnp.where(core == 0, stay, come), jnp.where(core == 0, come, stay)
    gain_part = gain_part + swap_core(gain_part)
    upper = lax.reduce_precision(gain_part, 8, 7)
    terms = jnp.concatenate([upper, gain_part - upper]).astype(jnp.bfloat16)
    extra = -(-2 * part // (16 * key_width)) * 16
    terms = jnp.pad(terms, (0, extra * key_width - 2 * part)).reshape(1, extra, key_width)
    key_rows = cores * capacity
    routed = jnp.concatenate(
        [
            jnp.stack([stay, come], axis=2).reshape(low, cores * key_rows, key_width),
            jnp.broadcast_to(terms, (low, extra, key_width)),
        ],
        axis=1,
    )
    if low == FEW:
        pieces = [lax.dynamic_index_in_dim(routed, lo ^ s, 0, keepdims=False) for s in range(low)]
        own = pieces[0]
        pieces[PIN], grad_terms = lax.optimization_barrier((pieces[PIN], grad_terms))
        for step in range(low):
            pairs = [
                ((h * low + j) * cores + c, ((h ^ c) * low + (j ^ step)) * cores + c)
                for h in range(halves)
                for j in range(low)
                for c in range(cores)
                if step or c
            ]
            pieces[step] = lax.ppermute(pieces[step], DP, pairs)
        pieces[0] = jnp.where(core == 0, own, pieces[0])
        pieces += [swap_core(piece) for piece in pieces]
        key_out, grad_gain = gather_pieces(pieces, norm_gain, key_rows, factor)
        grad_gain = grad_gain.reshape(width)
    else:
        routed = lax.all_to_all(
            jnp.concatenate(
                [whole_slots, jnp.broadcast_to(terms, (replicas, extra, key_width))], axis=1
            ),
            DP, split_axis=0, concat_axis=0, tiled=True)
        key_out = routed[:, :capacity].reshape(replicas * capacity, key_width)
        gain_sums = routed[:, capacity:].reshape(replicas, extra * key_width)[:, : 2 * part]
        gain_sums = gain_sums.astype(jnp.float32).reshape(halves, low, cores, 2, part)
        gain_sums = jnp.sum(gain_sums[:, :, 0], axis=(0, 2))
        grad_gain = gain_sums.reshape(width) * factor / norm_gain
    return (key_out[None], sum_terms(grad_terms, factor), grad_gain)


def solution(mesh):
    replicas, tensor = mesh.shape["dp"], mesh.shape["tensor"]
    split = Mesh(
        mesh.devices.reshape(2, replicas // 4, 2, tensor), ("hi", "lo", "core", "tensor")
    )
    return jax.shard_map(
        on_device,
        mesh=split,
        in_specs=(
            P(DP, "tensor"),
            P("tensor"),
            P(DP, "tensor"),
            P(DP, None, None),
            P(DP),
            P(DP),
        ),
        out_specs=(P(DP, None, None), P(DP, "tensor"), P("tensor")),
        check_vma=False,
    )
```

```python
import functools
import math

import jax
import jax.numpy as jnp
from jax import lax
from jax.experimental import pallas as pl
from jax.experimental.pallas import tpu as pltpu
from jax.sharding import Mesh
from jax.sharding import PartitionSpec as P

EPSILON = 1e-05

DP = ("hi", "lo", "core")
SWAP = [(0, 1), (1, 0)]
FEW = 4
PIN = 0
LANES = 128
CHUNK = 2048


def iota2(shape, dim):
    return lax.broadcasted_iota(jnp.int32, shape, dim)


def one_hot(index, size):
    return (index[:, None] == iota2((index.shape[0], size), 1)).astype(jnp.bfloat16)


def select(matrix, table):
    return jnp.dot(matrix, table, preferred_element_type=jnp.float32).astype(jnp.bfloat16)


def reduce_tensor(value):
    if lax.axis_size("tensor") == 2:
        return value + lax.ppermute(value, "tensor", SWAP)
    return lax.psum(value, "tensor")


def swap_core(value):
    return lax.ppermute(value, "core", SWAP)


def swap_lo(block):
    size, me = lax.axis_size("lo"), lax.axis_index("lo")
    if size <= FEW:
        pieces = [block(me)]
        for step in range(1, size):
            pairs = [(j, j ^ step) for j in range(size)]
            pieces.append(lax.ppermute(block(me ^ step), "lo", pairs))
        return pieces, [me ^ step for step in range(size)]
    sent = jnp.stack([block(j) for j in range(size)])
    got = lax.all_to_all(sent, "lo", split_axis=0, concat_axis=0, tiled=True)
    return [got.reshape((-1,) + got.shape[2:])], [jnp.int32(0)]


def slot_onehot(dest_rows, count, shards, capacity):
    rows = dest_rows.shape[0]
    same = (dest_rows[:, None] == dest_rows[None, :]) & (
        iota2((rows, rows), 1) < iota2((rows, rows), 0)
    )
    rank = jnp.sum(same.astype(jnp.int32), axis=1)
    accepted = lax.iota(jnp.int32, rows) < count
    position = jnp.where(accepted, dest_rows * capacity + rank, -1)
    return accepted, one_hot(position, shards * capacity)


def products_kernel(pieces, owned, core_keys, part, chunk, *refs):
    row_refs, weight_refs = refs[: 2 * pieces], refs[2 * pieces : 2 * pieces + 2]
    grad_ref, gain_ref = refs[2 * pieces + 2 : 2 * pieces + 4]
    key_refs = refs[2 * pieces + 4 : 3 * pieces + 4]
    rows_ref, cot_ref, weights_ref, sums_ref, row_sem, cot_sem, weight_sem = refs[
        3 * pieces + 4 :
    ]
    piece_rows = row_refs[0].shape[0]
    half_keys = core_keys // 2

    copies = []
    for j, ref in enumerate(row_refs):
        at = pl.ds(j * piece_rows, piece_rows)
        first = part + j // pieces * core_keys
        for source, to, sem in (
            (ref.at[:, pl.ds(0, part)], rows_ref, row_sem),
            (ref.at[:, pl.ds(first, core_keys)], cot_ref, cot_sem),
        ):
            copies.append(pltpu.make_async_copy(source, to.at[at], sem.at[j]))
    block = half_keys // pieces
    for j in range(2 * pieces):
        place = lax.axis_index("lo") ^ j % pieces if pieces > 1 else 0
        first = place * owned + (lax.axis_index("hi") ^ (j // pieces)) * half_keys
        if owned % 16 == 0:
            first = pl.multiple_of(first, 16)
        copies.append(
            pltpu.make_async_copy(
                weight_refs[j // pieces].at[pl.ds((j % pieces) * block, block)],
                weights_ref.at[pl.ds(first, block)],
                weight_sem.at[j],
            )
        )
    for copy in copies:
        copy.start()
    for copy in copies:
        copy.wait()

    for c in range(part // chunk):
        at = pl.ds(c * chunk, chunk)
        rows = rows_ref[:, at]
        weights = weights_ref[:, at]
        grad = lax.dot_general(
            cot_ref[...], rows, (((0,), (0,)), ((), ())), preferred_element_type=jnp.float32
        )
        grad_ref[:, at] = grad.astype(jnp.bfloat16)
        gain_ref[:, at] = jnp.sum(grad * weights.astype(jnp.float32), axis=0, keepdims=True)
        term = lax.dot_general(
            rows, weights, (((1,), (1,)), ((), ())), preferred_element_type=jnp.float32
        )
        if c == 0:
            sums_ref[...] = term
        else:
            sums_ref[...] += term
    for j, ref in enumerate(key_refs):
        for k in range(2):
            first = (k * pieces + j) * piece_rows
            ref[k] = sums_ref[first : first + piece_rows].astype(jnp.bfloat16)


def products(rows_here, rows_there, weights, core_keys, part, owned):
    pieces = len(rows_here)
    piece_rows, columns = rows_here[0].shape
    total = 2 * pieces * piece_rows
    return pl.pallas_call(
        functools.partial(
            products_kernel, pieces, owned, core_keys, part, min(CHUNK, part)
        ),
        out_shape=[
            jax.ShapeDtypeStruct((core_keys, part), jnp.bfloat16),
            jax.ShapeDtypeStruct((1, part), jnp.float32),
        ]
        + [jax.ShapeDtypeStruct((2, piece_rows, core_keys), jnp.bfloat16)] * pieces,
        in_specs=[pl.BlockSpec(memory_space=pl.ANY)] * (2 * pieces + 2),
        scratch_shapes=[
            pltpu.VMEM((total, part), jnp.bfloat16),
            pltpu.VMEM((total, core_keys), jnp.bfloat16),
            pltpu.VMEM((core_keys, part), jnp.bfloat16),
            pltpu.VMEM((total, core_keys), jnp.float32),
            pltpu.SemaphoreType.DMA((2 * pieces,)),
            pltpu.SemaphoreType.DMA((2 * pieces,)),
            pltpu.SemaphoreType.DMA((2 * pieces,)),
        ],
        compiler_params=pltpu.CompilerParams(vmem_limit_bytes=16 * 1024 * 1024),
        cost_estimate=pl.CostEstimate(
            flops=4 * total * core_keys * part,
            bytes_accessed=2 * total * columns + 8 * core_keys * part,
            transcendentals=0,
        ),
    )(*rows_here, *rows_there, *weights)


def sum_kernel(factor, terms_ref, grad_ref):
    low, _, part = terms_ref.shape[1:]
    for j in range(low):
        total = terms_ref[0, j].astype(jnp.float32) + terms_ref[1, j].astype(jnp.float32)
        grad_ref[:, pl.ds(j * part, part)] = total * factor


def sum_terms(terms, factor):
    _, low, owned, part = terms.shape
    return pl.pallas_call(
        functools.partial(sum_kernel, factor),
        out_shape=jax.ShapeDtypeStruct((owned, low * part), jnp.float32),
        in_specs=[pl.BlockSpec(memory_space=pltpu.VMEM)],
        out_specs=pl.BlockSpec(memory_space=pltpu.VMEM),
        compiler_params=pltpu.CompilerParams(vmem_limit_bytes=8 * 1024 * 1024),
        cost_estimate=pl.CostEstimate(
            flops=2 * terms.size, bytes_accessed=4 * terms.size, transcendentals=0
        ),
    )(terms)


def gather_kernel(key_rows, factor, *refs):
    pieces, norm_ref, key_ref, gain_ref = refs[:-3], refs[-3], refs[-2], refs[-1]
    low, columns = len(pieces) // 2, key_ref.shape[1]
    wide = columns // LANES
    half_rows = gain_ref.shape[0] // (low * wide)
    hi, lo, core = (lax.axis_index(name) for name in DP)
    mine = pl.ds(pl.multiple_of(core * key_rows, key_rows), key_rows)
    for step in range(low):
        place = lo ^ step
        total = jnp.zeros((half_rows, columns), jnp.float32)
        for k in range(2):
            piece = pieces[k * low + step]
            at = ((hi ^ core ^ k) * low + place) * key_rows
            key_ref[pl.ds(pl.multiple_of(at, key_rows), key_rows)] = piece[mine]
            terms = piece[2 * key_rows :].astype(jnp.float32)
            total = total + terms[:half_rows] + terms[half_rows : 2 * half_rows]
        for i in range(half_rows):
            for j in range(wide):
                at = pl.ds((place * half_rows + i) * wide + j, 1)
                sums = total[i : i + 1, j * LANES : (j + 1) * LANES]
                gain_ref[at] = sums * factor / norm_ref[at]


def gather_pieces(pieces, norm_gain, key_rows, factor):
    key_width, width = pieces[0].shape[1], norm_gain.shape[0]
    return pl.pallas_call(
        functools.partial(gather_kernel, key_rows, factor),
        out_shape=[
            jax.ShapeDtypeStruct((len(pieces) * key_rows, key_width), jnp.bfloat16),
            jax.ShapeDtypeStruct((width // LANES, LANES), jnp.float32),
        ],
        in_specs=[pl.BlockSpec(memory_space=pltpu.VMEM)] * (len(pieces) + 1),
        out_specs=[pl.BlockSpec(memory_space=pltpu.VMEM)] * 2,
        compiler_params=pltpu.CompilerParams(vmem_limit_bytes=4 * 1024 * 1024),
    )(*pieces, norm_gain.reshape(width // LANES, LANES))


def on_device(hidden_rows, norm_gain, key_weight, cotangent, accepted_counts, destination):
    halves, low, cores = lax.axis_size("hi"), lax.axis_size("lo"), lax.axis_size("core")
    hi, lo, core = (lax.axis_index(name) for name in DP)
    replicas = halves * low * cores
    rows, width = hidden_rows.shape
    model_width = width * lax.axis_size("tensor")
    owned, key_width = key_weight.shape[0], cotangent.shape[2]
    part = width // low
    core_keys = key_width // cores
    capacity = cotangent.shape[1] // replicas
    factor = 1.0 / math.sqrt(rows * replicas)

    weight_here, places = swap_lo(
        lambda j: lax.dynamic_slice(key_weight, (0, j * part), (owned, part))
    )
    weight_here = jnp.concatenate(weight_here)
    weight_there = lax.ppermute(weight_here, "hi", SWAP)

    returned = lax.all_to_all(cotangent[0], DP, split_axis=0, concat_axis=0, tiled=True)
    accepted, onehot = slot_onehot(destination, accepted_counts[0], replicas, capacity)
    place = lax.iota(jnp.int32, key_width)
    from_core = core ^ (place // core_keys)
    whole = ((place % core_keys) // owned * cores + from_core) * owned + place % owned
    by_core = one_hot(whole, key_width)
    row_cot = lax.dot_general(
        select(onehot, returned),
        by_core,
        (((1,), (1,)), ((), ())),
        preferred_element_type=jnp.float32,
    ).astype(jnp.bfloat16)

    row_float = hidden_rows.astype(jnp.float32)
    squares = jnp.sum(row_float * row_float, axis=1)
    scale = lax.rsqrt(reduce_tensor(squares) / model_width + EPSILON)
    normed = jnp.where(
        accepted[:, None], row_float * scale[:, None] * norm_gain[None, :], jnp.float32(0.0)
    ).astype(jnp.bfloat16)

    rows_here, _ = swap_lo(
        lambda j: jnp.concatenate(
            [lax.dynamic_slice(normed, (0, j * part), (rows, part)), row_cot], axis=1
        )
    )
    rows_there = [swap_core(piece) for piece in rows_here]
    grad_part, gain_part, *key_parts = products(
        rows_here, rows_there, (weight_here, weight_there), core_keys, part, owned
    )
    gain_part = gain_part[0]

    if low <= FEW:
        key_terms = [key_parts[0]] + [
            lax.ppermute(key_parts[step], "lo", [(j, j ^ step) for j in range(low)])
            for step in range(1, low)
        ]
    else:
        sent = key_parts[0].reshape(2, low, rows, core_keys).transpose(1, 0, 2, 3)
        got = lax.all_to_all(sent, "lo", split_axis=0, concat_axis=0, tiled=True)
        key_terms = [got[j] for j in range(low)]
    grad_terms = lax.all_to_all(
        grad_part.reshape(halves * low, owned, part),
        ("hi", "lo"),
        split_axis=0,
        concat_axis=0,
        tiled=True,
    ).reshape(halves, low, owned, part)
    key_sum = sum(term.astype(jnp.float32) for term in key_terms)
    chip_keys = reduce_tensor(key_sum).astype(jnp.bfloat16)
    row_keys = jnp.concatenate([chip_keys[0], swap_core(chip_keys[1])], axis=1)
    key_slots = lax.dot_general(
        onehot, row_keys, (((0,), (0,)), ((), ())), preferred_element_type=jnp.float32
    ).astype(jnp.bfloat16)
    key_slots = select(key_slots, by_core)

    whole_slots = key_slots.reshape(replicas, capacity, key_width)
    key_slots = key_slots.reshape(halves, low, cores, capacity, key_width)
    stay = lax.dynamic_index_in_dim(key_slots, hi ^ core, 0, keepdims=False)
    come = swap_core(lax.dynamic_index_in_dim(key_slots, hi ^ 1 ^ core, 0, keepdims=False))
    stay, come = jnp.where(core == 0, stay, come), jnp.where(core == 0, come, stay)
    gain_part = gain_part + swap_core(gain_part)
    upper = lax.reduce_precision(gain_part, 8, 7)
    terms = jnp.concatenate([upper, gain_part - upper]).astype(jnp.bfloat16)
    extra = -(-2 * part // (16 * key_width)) * 16
    terms = jnp.pad(terms, (0, extra * key_width - 2 * part)).reshape(1, extra, key_width)
    key_rows = cores * capacity
    routed = jnp.concatenate(
        [
            jnp.stack([stay, come], axis=2).reshape(low, cores * key_rows, key_width),
            jnp.broadcast_to(terms, (low, extra, key_width)),
        ],
        axis=1,
    )
    if low == FEW:
        pieces = [lax.dynamic_index_in_dim(routed, lo ^ s, 0, keepdims=False) for s in range(low)]
        own = pieces[0]
        pieces[PIN], grad_terms = lax.optimization_barrier((pieces[PIN], grad_terms))
        for step in range(low):
            pairs = [
                ((h * low + j) * cores + c, ((h ^ c) * low + (j ^ step)) * cores + c)
                for h in range(halves)
                for j in range(low)
                for c in range(cores)
                if step or c
            ]
            pieces[step] = lax.ppermute(pieces[step], DP, pairs)
        pieces[0] = jnp.where(core == 0, own, pieces[0])
        pieces += [swap_core(piece) for piece in pieces]
        key_out, grad_gain = gather_pieces(pieces, norm_gain, key_rows, factor)
        grad_gain = grad_gain.reshape(width)
    else:
        routed = lax.all_to_all(
            jnp.concatenate(
                [whole_slots, jnp.broadcast_to(terms, (replicas, extra, key_width))], axis=1
            ),
            DP, split_axis=0, concat_axis=0, tiled=True)
        key_out = routed[:, :capacity].reshape(replicas * capacity, key_width)
        gain_sums = routed[:, capacity:].reshape(replicas, extra * key_width)[:, : 2 * part]
        gain_sums = gain_sums.astype(jnp.float32).reshape(halves, low, cores, 2, part)
        gain_sums = jnp.sum(gain_sums[:, :, 0], axis=(0, 2))
        grad_gain = gain_sums.reshape(width) * factor / norm_gain
    return (key_out[None], sum_terms(grad_terms, factor), grad_gain)


def solution(mesh):
    replicas, tensor = mesh.shape["dp"], mesh.shape["tensor"]
    split = Mesh(
        mesh.devices.reshape(2, replicas // 4, 2, tensor), ("hi", "lo", "core", "tensor")
    )
    return jax.shard_map(
        on_device,
        mesh=split,
        in_specs=(
            P(DP, "tensor"),
            P("tensor"),
            P(DP, "tensor"),
            P(DP, None, None),
            P(DP),
            P(DP),
        ),
        out_specs=(P(DP, None, None), P(DP, "tensor"), P("tensor")),
        check_vma=False,
    )
```

```python
import functools
import math

import jax
import jax.numpy as jnp
from jax import lax
from jax.experimental import pallas as pl
from jax.experimental.pallas import tpu as pltpu
from jax.sharding import Mesh
from jax.sharding import PartitionSpec as P

EPSILON = 1e-05

DP = ("hi", "lo", "core")
SWAP = [(0, 1), (1, 0)]
FEW = 4
PIN = 0
LANES = 128
CHUNK = 2048


def iota2(shape, dim):
    return lax.broadcasted_iota(jnp.int32, shape, dim)


def one_hot(index, size):
    return (index[:, None] == iota2((index.shape[0], size), 1)).astype(jnp.bfloat16)


def select(matrix, table):
    return jnp.dot(matrix, table, preferred_element_type=jnp.float32).astype(jnp.bfloat16)


def reduce_tensor(value):
    if lax.axis_size("tensor") == 2:
        return value + lax.ppermute(value, "tensor", SWAP)
    return lax.psum(value, "tensor")


def swap_core(value):
    return lax.ppermute(value, "core", SWAP)


def swap_lo(block):
    size, me = lax.axis_size("lo"), lax.axis_index("lo")
    if size <= FEW:
        pieces = [block(me)]
        for step in range(1, size):
            pairs = [(j, j ^ step) for j in range(size)]
            pieces.append(lax.ppermute(block(me ^ step), "lo", pairs))
        return pieces, [me ^ step for step in range(size)]
    sent = jnp.stack([block(j) for j in range(size)])
    got = lax.all_to_all(sent, "lo", split_axis=0, concat_axis=0, tiled=True)
    return [got.reshape((-1,) + got.shape[2:])], [jnp.int32(0)]


def slot_onehot(dest_rows, count, shards, capacity):
    rows = dest_rows.shape[0]
    same = (dest_rows[:, None] == dest_rows[None, :]) & (
        iota2((rows, rows), 1) < iota2((rows, rows), 0)
    )
    rank = jnp.sum(same.astype(jnp.int32), axis=1)
    accepted = lax.iota(jnp.int32, rows) < count
    position = jnp.where(accepted, dest_rows * capacity + rank, -1)
    return accepted, one_hot(position, shards * capacity)


def products_kernel(pieces, owned, core_keys, part, chunk, *refs):
    row_refs, weight_refs = refs[: 2 * pieces], refs[2 * pieces : 2 * pieces + 2]
    grad_ref, gain_ref = refs[2 * pieces + 2 : 2 * pieces + 4]
    key_refs = refs[2 * pieces + 4 : 3 * pieces + 4]
    rows_ref, cot_ref, weights_ref, sums_ref, row_sem, cot_sem, weight_sem = refs[
        3 * pieces + 4 :
    ]
    piece_rows = row_refs[0].shape[0]
    half_keys = core_keys // 2

    copies = []
    for j, ref in enumerate(row_refs):
        at = pl.ds(j * piece_rows, piece_rows)
        first = part + j // pieces * core_keys
        for source, to, sem in (
            (ref.at[:, pl.ds(0, part)], rows_ref, row_sem),
            (ref.at[:, pl.ds(first, core_keys)], cot_ref, cot_sem),
        ):
            copies.append(pltpu.make_async_copy(source, to.at[at], sem.at[j]))
    block = half_keys // pieces
    for j in range(2 * pieces):
        place = lax.axis_index("lo") ^ j % pieces if pieces > 1 else 0
        first = place * owned + (lax.axis_index("hi") ^ (j // pieces)) * half_keys
        if owned % 16 == 0:
            first = pl.multiple_of(first, 16)
        copies.append(
            pltpu.make_async_copy(
                weight_refs[j // pieces].at[pl.ds((j % pieces) * block, block)],
                weights_ref.at[pl.ds(first, block)],
                weight_sem.at[j],
            )
        )
    for copy in copies:
        copy.start()
    for copy in copies:
        copy.wait()

    for c in range(part // chunk):
        at = pl.ds(c * chunk, chunk)
        rows = rows_ref[:, at]
        weights = weights_ref[:, at]
        grad = lax.dot_general(
            cot_ref[...], rows, (((0,), (0,)), ((), ())), preferred_element_type=jnp.float32
        )
        grad_ref[:, at] = grad.astype(jnp.bfloat16)
        gain_ref[:, at] = jnp.sum(grad * weights.astype(jnp.float32), axis=0, keepdims=True)
        term = lax.dot_general(
            rows, weights, (((1,), (1,)), ((), ())), preferred_element_type=jnp.float32
        )
        if c == 0:
            sums_ref[...] = term
        else:
            sums_ref[...] += term
    for j, ref in enumerate(key_refs):
        for k in range(2):
            first = (k * pieces + j) * piece_rows
            ref[k] = sums_ref[first : first + piece_rows].astype(jnp.bfloat16)


def products(rows_here, rows_there, weights, core_keys, part, owned):
    pieces = len(rows_here)
    piece_rows, columns = rows_here[0].shape
    total = 2 * pieces * piece_rows
    return pl.pallas_call(
        functools.partial(
            products_kernel, pieces, owned, core_keys, part, min(CHUNK, part)
        ),
        out_shape=[
            jax.ShapeDtypeStruct((core_keys, part), jnp.bfloat16),
            jax.ShapeDtypeStruct((1, part), jnp.float32),
        ]
        + [jax.ShapeDtypeStruct((2, piece_rows, core_keys), jnp.bfloat16)] * pieces,
        in_specs=[pl.BlockSpec(memory_space=pl.ANY)] * (2 * pieces + 2),
        scratch_shapes=[
            pltpu.VMEM((total, part), jnp.bfloat16),
            pltpu.VMEM((total, core_keys), jnp.bfloat16),
            pltpu.VMEM((core_keys, part), jnp.bfloat16),
            pltpu.VMEM((total, core_keys), jnp.float32),
            pltpu.SemaphoreType.DMA((2 * pieces,)),
            pltpu.SemaphoreType.DMA((2 * pieces,)),
            pltpu.SemaphoreType.DMA((2 * pieces,)),
        ],
        compiler_params=pltpu.CompilerParams(vmem_limit_bytes=24 * 1024 * 1024),
        cost_estimate=pl.CostEstimate(
            flops=4 * total * core_keys * part,
            bytes_accessed=2 * total * columns + 8 * core_keys * part,
            transcendentals=0,
        ),
    )(*rows_here, *rows_there, *weights)


def sum_kernel(factor, terms_ref, grad_ref):
    low, _, part = terms_ref.shape[1:]
    for j in range(low):
        total = terms_ref[0, j].astype(jnp.float32) + terms_ref[1, j].astype(jnp.float32)
        grad_ref[:, pl.ds(j * part, part)] = total * factor


def sum_terms(terms, factor):
    _, low, owned, part = terms.shape
    return pl.pallas_call(
        functools.partial(sum_kernel, factor),
        out_shape=jax.ShapeDtypeStruct((owned, low * part), jnp.float32),
        in_specs=[pl.BlockSpec(memory_space=pltpu.VMEM)],
        out_specs=pl.BlockSpec(memory_space=pltpu.VMEM),
        compiler_params=pltpu.CompilerParams(vmem_limit_bytes=4 * 1024 * 1024),
        cost_estimate=pl.CostEstimate(
            flops=2 * terms.size, bytes_accessed=4 * terms.size, transcendentals=0
        ),
    )(terms)


def gather_kernel(key_rows, factor, *refs):
    pieces, norm_ref, key_ref, gain_ref = refs[:-3], refs[-3], refs[-2], refs[-1]
    low, columns = len(pieces) // 2, key_ref.shape[1]
    wide = columns // LANES
    half_rows = gain_ref.shape[0] // (low * wide)
    hi, lo, core = (lax.axis_index(name) for name in DP)
    mine = pl.ds(pl.multiple_of(core * key_rows, key_rows), key_rows)
    for step in range(low):
        place = lo ^ step
        total = jnp.zeros((half_rows, columns), jnp.float32)
        for k in range(2):
            piece = pieces[k * low + step]
            at = ((hi ^ core ^ k) * low + place) * key_rows
            key_ref[pl.ds(pl.multiple_of(at, key_rows), key_rows)] = piece[mine]
            terms = piece[2 * key_rows :].astype(jnp.float32)
            total = total + terms[:half_rows] + terms[half_rows : 2 * half_rows]
        for i in range(half_rows):
            for j in range(wide):
                at = pl.ds((place * half_rows + i) * wide + j, 1)
                sums = total[i : i + 1, j * LANES : (j + 1) * LANES]
                gain_ref[at] = sums * factor / norm_ref[at]


def gather_pieces(pieces, norm_gain, key_rows, factor):
    key_width, width = pieces[0].shape[1], norm_gain.shape[0]
    return pl.pallas_call(
        functools.partial(gather_kernel, key_rows, factor),
        out_shape=[
            jax.ShapeDtypeStruct((len(pieces) * key_rows, key_width), jnp.bfloat16),
            jax.ShapeDtypeStruct((width // LANES, LANES), jnp.float32),
        ],
        in_specs=[pl.BlockSpec(memory_space=pltpu.VMEM)] * (len(pieces) + 1),
        out_specs=[pl.BlockSpec(memory_space=pltpu.VMEM)] * 2,
        compiler_params=pltpu.CompilerParams(vmem_limit_bytes=4 * 1024 * 1024),
    )(*pieces, norm_gain.reshape(width // LANES, LANES))


def on_device(hidden_rows, norm_gain, key_weight, cotangent, accepted_counts, destination):
    halves, low, cores = lax.axis_size("hi"), lax.axis_size("lo"), lax.axis_size("core")
    hi, lo, core = (lax.axis_index(name) for name in DP)
    replicas = halves * low * cores
    rows, width = hidden_rows.shape
    model_width = width * lax.axis_size("tensor")
    owned, key_width = key_weight.shape[0], cotangent.shape[2]
    part = width // low
    core_keys = key_width // cores
    capacity = cotangent.shape[1] // replicas
    factor = 1.0 / math.sqrt(rows * replicas)

    weight_here, places = swap_lo(
        lambda j: lax.dynamic_slice(key_weight, (0, j * part), (owned, part))
    )
    weight_here = jnp.concatenate(weight_here)
    weight_there = lax.ppermute(weight_here, "hi", SWAP)

    returned = lax.all_to_all(cotangent[0], DP, split_axis=0, concat_axis=0, tiled=True)
    accepted, onehot = slot_onehot(destination, accepted_counts[0], replicas, capacity)
    place = lax.iota(jnp.int32, key_width)
    from_core = core ^ (place // core_keys)
    whole = ((place % core_keys) // owned * cores + from_core) * owned + place % owned
    by_core = one_hot(whole, key_width)
    row_cot = lax.dot_general(
        select(onehot, returned),
        by_core,
        (((1,), (1,)), ((), ())),
        preferred_element_type=jnp.float32,
    ).astype(jnp.bfloat16)

    row_float = hidden_rows.astype(jnp.float32)
    squares = jnp.sum(row_float * row_float, axis=1)
    scale = lax.rsqrt(reduce_tensor(squares) / model_width + EPSILON)
    normed = jnp.where(
        accepted[:, None], row_float * scale[:, None] * norm_gain[None, :], jnp.float32(0.0)
    ).astype(jnp.bfloat16)

    rows_here, _ = swap_lo(
        lambda j: jnp.concatenate(
            [lax.dynamic_slice(normed, (0, j * part), (rows, part)), row_cot], axis=1
        )
    )
    rows_there = [swap_core(piece) for piece in rows_here]
    grad_part, gain_part, *key_parts = products(
        rows_here, rows_there, (weight_here, weight_there), core_keys, part, owned
    )
    gain_part = gain_part[0]

    if low <= FEW:
        key_terms = [key_parts[0]] + [
            lax.ppermute(key_parts[step], "lo", [(j, j ^ step) for j in range(low)])
            for step in range(1, low)
        ]
    else:
        sent = key_parts[0].reshape(2, low, rows, core_keys).transpose(1, 0, 2, 3)
        got = lax.all_to_all(sent, "lo", split_axis=0, concat_axis=0, tiled=True)
        key_terms = [got[j] for j in range(low)]
    grad_terms = lax.all_to_all(
        grad_part.reshape(halves * low, owned, part),
        ("hi", "lo"),
        split_axis=0,
        concat_axis=0,
        tiled=True,
    ).reshape(halves, low, owned, part)
    key_sum = sum(term.astype(jnp.float32) for term in key_terms)
    chip_keys = reduce_tensor(key_sum).astype(jnp.bfloat16)
    row_keys = jnp.concatenate([chip_keys[0], swap_core(chip_keys[1])], axis=1)
    key_slots = lax.dot_general(
        onehot, row_keys, (((0,), (0,)), ((), ())), preferred_element_type=jnp.float32
    ).astype(jnp.bfloat16)
    key_slots = select(key_slots, by_core)

    whole_slots = key_slots.reshape(replicas, capacity, key_width)
    key_slots = key_slots.reshape(halves, low, cores, capacity, key_width)
    stay = lax.dynamic_index_in_dim(key_slots, hi ^ core, 0, keepdims=False)
    come = swap_core(lax.dynamic_index_in_dim(key_slots, hi ^ 1 ^ core, 0, keepdims=False))
    stay, come = jnp.where(core == 0, stay, come), jnp.where(core == 0, come, stay)
    gain_part = gain_part + swap_core(gain_part)
    upper = lax.reduce_precision(gain_part, 8, 7)
    terms = jnp.concatenate([upper, gain_part - upper]).astype(jnp.bfloat16)
    extra = -(-2 * part // (16 * key_width)) * 16
    terms = jnp.pad(terms, (0, extra * key_width - 2 * part)).reshape(1, extra, key_width)
    key_rows = cores * capacity
    routed = jnp.concatenate(
        [
            jnp.stack([stay, come], axis=2).reshape(low, cores * key_rows, key_width),
            jnp.broadcast_to(terms, (low, extra, key_width)),
        ],
        axis=1,
    )
    if low == FEW:
        pieces = [lax.dynamic_index_in_dim(routed, lo ^ s, 0, keepdims=False) for s in range(low)]
        own = pieces[0]
        pieces[PIN], grad_terms = lax.optimization_barrier((pieces[PIN], grad_terms))
        for step in range(low):
            pairs = [
                ((h * low + j) * cores + c, ((h ^ c) * low + (j ^ step)) * cores + c)
                for h in range(halves)
                for j in range(low)
                for c in range(cores)
                if step or c
            ]
            pieces[step] = lax.ppermute(pieces[step], DP, pairs)
        pieces[0] = jnp.where(core == 0, own, pieces[0])
        pieces += [swap_core(piece) for piece in pieces]
        key_out, grad_gain = gather_pieces(pieces, norm_gain, key_rows, factor)
        grad_gain = grad_gain.reshape(width)
    else:
        routed = lax.all_to_all(
            jnp.concatenate(
                [whole_slots, jnp.broadcast_to(terms, (replicas, extra, key_width))], axis=1
            ),
            DP, split_axis=0, concat_axis=0, tiled=True)
        key_out = routed[:, :capacity].reshape(replicas * capacity, key_width)
        gain_sums = routed[:, capacity:].reshape(replicas, extra * key_width)[:, : 2 * part]
        gain_sums = gain_sums.astype(jnp.float32).reshape(halves, low, cores, 2, part)
        gain_sums = jnp.sum(gain_sums[:, :, 0], axis=(0, 2))
        grad_gain = gain_sums.reshape(width) * factor / norm_gain
    return (key_out[None], sum_terms(grad_terms, factor), grad_gain)


def solution(mesh):
    replicas, tensor = mesh.shape["dp"], mesh.shape["tensor"]
    split = Mesh(
        mesh.devices.reshape(2, replicas // 4, 2, tensor), ("hi", "lo", "core", "tensor")
    )
    return jax.shard_map(
        on_device,
        mesh=split,
        in_specs=(
            P(DP, "tensor"),
            P("tensor"),
            P(DP, "tensor"),
            P(DP, None, None),
            P(DP),
            P(DP),
        ),
        out_specs=(P(DP, None, None), P(DP, "tensor"), P("tensor")),
        check_vma=False,
    )
```

```python
import functools
import math

import jax
import jax.numpy as jnp
from jax import lax
from jax.experimental import pallas as pl
from jax.experimental.pallas import tpu as pltpu
from jax.sharding import Mesh
from jax.sharding import PartitionSpec as P

EPSILON = 1e-05

DP = ("hi", "lo", "core")
SWAP = [(0, 1), (1, 0)]
FEW = 4
PIN = 0
LANES = 128
CHUNK = 2048


def iota2(shape, dim):
    return lax.broadcasted_iota(jnp.int32, shape, dim)


def one_hot(index, size):
    return (index[:, None] == iota2((index.shape[0], size), 1)).astype(jnp.bfloat16)


def select(matrix, table):
    return jnp.dot(matrix, table, preferred_element_type=jnp.float32).astype(jnp.bfloat16)


def reduce_tensor(value):
    if lax.axis_size("tensor") == 2:
        return value + lax.ppermute(value, "tensor", SWAP)
    return lax.psum(value, "tensor")


def swap_core(value):
    return lax.ppermute(value, "core", SWAP)


def swap_lo(block):
    size, me = lax.axis_size("lo"), lax.axis_index("lo")
    if size <= FEW:
        pieces = [block(me)]
        for step in range(1, size):
            pairs = [(j, j ^ step) for j in range(size)]
            pieces.append(lax.ppermute(block(me ^ step), "lo", pairs))
        return pieces, [me ^ step for step in range(size)]
    sent = jnp.stack([block(j) for j in range(size)])
    got = lax.all_to_all(sent, "lo", split_axis=0, concat_axis=0, tiled=True)
    return [got.reshape((-1,) + got.shape[2:])], [jnp.int32(0)]


def slot_onehot(dest_rows, count, shards, capacity):
    rows = dest_rows.shape[0]
    same = (dest_rows[:, None] == dest_rows[None, :]) & (
        iota2((rows, rows), 1) < iota2((rows, rows), 0)
    )
    rank = jnp.sum(same.astype(jnp.int32), axis=1)
    accepted = lax.iota(jnp.int32, rows) < count
    position = jnp.where(accepted, dest_rows * capacity + rank, -1)
    return accepted, one_hot(position, shards * capacity)


def products_kernel(pieces, owned, core_keys, part, chunk, *refs):
    row_refs, weight_refs = refs[: 2 * pieces], refs[2 * pieces : 2 * pieces + 2]
    grad_ref, gain_ref = refs[2 * pieces + 2 : 2 * pieces + 4]
    key_refs = refs[2 * pieces + 4 : 3 * pieces + 4]
    rows_ref, cot_ref, weights_ref, sums_ref, row_sem, cot_sem, weight_sem = refs[
        3 * pieces + 4 :
    ]
    piece_rows = row_refs[0].shape[0]
    half_keys = core_keys // 2

    copies = []
    for j, ref in enumerate(row_refs):
        at = pl.ds(j * piece_rows, piece_rows)
        first = part + j // pieces * core_keys
        for source, to, sem in (
            (ref.at[:, pl.ds(0, part)], rows_ref, row_sem),
            (ref.at[:, pl.ds(first, core_keys)], cot_ref, cot_sem),
        ):
            copies.append(pltpu.make_async_copy(source, to.at[at], sem.at[j]))
    block = half_keys // pieces
    for j in range(2 * pieces):
        place = lax.axis_index("lo") ^ j % pieces if pieces > 1 else 0
        first = place * owned + (lax.axis_index("hi") ^ (j // pieces)) * half_keys
        if owned % 16 == 0:
            first = pl.multiple_of(first, 16)
        copies.append(
            pltpu.make_async_copy(
                weight_refs[j // pieces].at[pl.ds((j % pieces) * block, block)],
                weights_ref.at[pl.ds(first, block)],
                weight_sem.at[j],
            )
        )
    for copy in copies:
        copy.start()
    for copy in copies:
        copy.wait()

    for c in range(part // chunk):
        at = pl.ds(c * chunk, chunk)
        rows = rows_ref[:, at]
        weights = weights_ref[:, at]
        grad = lax.dot_general(
            cot_ref[...], rows, (((0,), (0,)), ((), ())), preferred_element_type=jnp.float32
        )
        grad_ref[:, at] = grad.astype(jnp.bfloat16)
        gain_ref[:, at] = jnp.sum(grad * weights.astype(jnp.float32), axis=0, keepdims=True)
        term = lax.dot_general(
            rows, weights, (((1,), (1,)), ((), ())), preferred_element_type=jnp.float32
        )
        if c == 0:
            sums_ref[...] = term
        else:
            sums_ref[...] += term
    for j, ref in enumerate(key_refs):
        for k in range(2):
            first = (k * pieces + j) * piece_rows
            ref[k] = sums_ref[first : first + piece_rows].astype(jnp.bfloat16)


def products(rows_here, rows_there, weights, core_keys, part, owned):
    pieces = len(rows_here)
    piece_rows, columns = rows_here[0].shape
    total = 2 * pieces * piece_rows
    return pl.pallas_call(
        functools.partial(
            products_kernel, pieces, owned, core_keys, part, min(CHUNK, part)
        ),
        out_shape=[
            jax.ShapeDtypeStruct((core_keys, part), jnp.bfloat16),
            jax.ShapeDtypeStruct((1, part), jnp.float32),
        ]
        + [jax.ShapeDtypeStruct((2, piece_rows, core_keys), jnp.bfloat16)] * pieces,
        in_specs=[pl.BlockSpec(memory_space=pl.ANY)] * (2 * pieces + 2),
        scratch_shapes=[
            pltpu.VMEM((total, part), jnp.bfloat16),
            pltpu.VMEM((total, core_keys), jnp.bfloat16),
            pltpu.VMEM((core_keys, part), jnp.bfloat16),
            pltpu.VMEM((total, core_keys), jnp.float32),
            pltpu.SemaphoreType.DMA((2 * pieces,)),
            pltpu.SemaphoreType.DMA((2 * pieces,)),
            pltpu.SemaphoreType.DMA((2 * pieces,)),
        ],
        compiler_params=pltpu.CompilerParams(vmem_limit_bytes=16 * 1024 * 1024),
        cost_estimate=pl.CostEstimate(
            flops=4 * total * core_keys * part,
            bytes_accessed=2 * total * columns + 8 * core_keys * part,
            transcendentals=0,
        ),
    )(*rows_here, *rows_there, *weights)


def sum_kernel(factor, terms_ref, grad_ref):
    low, _, part = terms_ref.shape[1:]
    for j in range(low):
        total = terms_ref[0, j].astype(jnp.float32) + terms_ref[1, j].astype(jnp.float32)
        grad_ref[:, pl.ds(j * part, part)] = total * factor


def sum_terms(terms, factor):
    _, low, owned, part = terms.shape
    return pl.pallas_call(
        functools.partial(sum_kernel, factor),
        out_shape=jax.ShapeDtypeStruct((owned, low * part), jnp.float32),
        in_specs=[pl.BlockSpec(memory_space=pltpu.VMEM)],
        out_specs=pl.BlockSpec(memory_space=pltpu.VMEM),
        compiler_params=pltpu.CompilerParams(vmem_limit_bytes=8 * 1024 * 1024),
        cost_estimate=pl.CostEstimate(
            flops=2 * terms.size, bytes_accessed=4 * terms.size, transcendentals=0
        ),
    )(terms)


def gather_kernel(key_rows, factor, *refs):
    pieces, norm_ref, key_ref, gain_ref = refs[:-3], refs[-3], refs[-2], refs[-1]
    low, columns = len(pieces) // 2, key_ref.shape[1]
    wide = columns // LANES
    half_rows = gain_ref.shape[0] // (low * wide)
    hi, lo, core = (lax.axis_index(name) for name in DP)
    mine = pl.ds(pl.multiple_of(core * key_rows, key_rows), key_rows)
    for step in range(low):
        place = lo ^ step
        total = jnp.zeros((half_rows, columns), jnp.float32)
        for k in range(2):
            piece = pieces[k * low + step]
            at = ((hi ^ core ^ k) * low + place) * key_rows
            key_ref[pl.ds(pl.multiple_of(at, key_rows), key_rows)] = piece[mine]
            terms = piece[2 * key_rows :].astype(jnp.float32)
            total = total + terms[:half_rows] + terms[half_rows : 2 * half_rows]
        for i in range(half_rows):
            for j in range(wide):
                at = pl.ds((place * half_rows + i) * wide + j, 1)
                sums = total[i : i + 1, j * LANES : (j + 1) * LANES]
                gain_ref[at] = sums * factor / norm_ref[at]


def gather_pieces(pieces, norm_gain, key_rows, factor):
    key_width, width = pieces[0].shape[1], norm_gain.shape[0]
    return pl.pallas_call(
        functools.partial(gather_kernel, key_rows, factor),
        out_shape=[
            jax.ShapeDtypeStruct((len(pieces) * key_rows, key_width), jnp.bfloat16),
            jax.ShapeDtypeStruct((width // LANES, LANES), jnp.float32),
        ],
        in_specs=[pl.BlockSpec(memory_space=pltpu.VMEM)] * (len(pieces) + 1),
        out_specs=[pl.BlockSpec(memory_space=pltpu.VMEM)] * 2,
        compiler_params=pltpu.CompilerParams(vmem_limit_bytes=4 * 1024 * 1024),
    )(*pieces, norm_gain.reshape(width // LANES, LANES))


def on_device(hidden_rows, norm_gain, key_weight, cotangent, accepted_counts, destination):
    halves, low, cores = lax.axis_size("hi"), lax.axis_size("lo"), lax.axis_size("core")
    hi, lo, core = (lax.axis_index(name) for name in DP)
    replicas = halves * low * cores
    rows, width = hidden_rows.shape
    model_width = width * lax.axis_size("tensor")
    owned, key_width = key_weight.shape[0], cotangent.shape[2]
    part = width // low
    core_keys = key_width // cores
    capacity = cotangent.shape[1] // replicas
    factor = 1.0 / math.sqrt(rows * replicas)

    weight_here, places = swap_lo(
        lambda j: lax.dynamic_slice(key_weight, (0, j * part), (owned, part))
    )
    weight_here = jnp.concatenate(weight_here)
    weight_there = lax.ppermute(weight_here, "hi", SWAP)

    returned = lax.all_to_all(cotangent[0], DP, split_axis=0, concat_axis=0, tiled=True)
    accepted, onehot = slot_onehot(destination, accepted_counts[0], replicas, capacity)
    place = lax.iota(jnp.int32, key_width)
    from_core = core ^ (place // core_keys)
    whole = ((place % core_keys) // owned * cores + from_core) * owned + place % owned
    by_core = one_hot(whole, key_width)
    row_cot = lax.dot_general(
        select(onehot, returned),
        by_core,
        (((1,), (1,)), ((), ())),
        preferred_element_type=jnp.float32,
    ).astype(jnp.bfloat16)

    row_float = hidden_rows.astype(jnp.float32)
    squares = jnp.sum(row_float * row_float, axis=1)
    scale = lax.rsqrt(reduce_tensor(squares) / model_width + EPSILON)
    normed = jnp.where(
        accepted[:, None], row_float * scale[:, None] * norm_gain[None, :], jnp.float32(0.0)
    ).astype(jnp.bfloat16)

    rows_here, _ = swap_lo(
        lambda j: jnp.concatenate(
            [lax.dynamic_slice(normed, (0, j * part), (rows, part)), row_cot], axis=1
        )
    )
    rows_there = [swap_core(piece) for piece in rows_here[::-1]][::-1]
    grad_part, gain_part, *key_parts = products(
        rows_here, rows_there, (weight_here, weight_there), core_keys, part, owned
    )
    gain_part = gain_part[0]

    if low <= FEW:
        key_terms = [key_parts[0]] + [
            lax.ppermute(key_parts[step], "lo", [(j, j ^ step) for j in range(low)])
            for step in range(1, low)
        ]
    else:
        sent = key_parts[0].reshape(2, low, rows, core_keys).transpose(1, 0, 2, 3)
        got = lax.all_to_all(sent, "lo", split_axis=0, concat_axis=0, tiled=True)
        key_terms = [got[j] for j in range(low)]
    grad_terms = lax.all_to_all(
        grad_part.reshape(halves * low, owned, part),
        ("hi", "lo"),
        split_axis=0,
        concat_axis=0,
        tiled=True,
    ).reshape(halves, low, owned, part)
    key_sum = sum(term.astype(jnp.float32) for term in key_terms)
    chip_keys = reduce_tensor(key_sum).astype(jnp.bfloat16)
    row_keys = jnp.concatenate([chip_keys[0], swap_core(chip_keys[1])], axis=1)
    key_slots = lax.dot_general(
        onehot, row_keys, (((0,), (0,)), ((), ())), preferred_element_type=jnp.float32
    ).astype(jnp.bfloat16)
    key_slots = select(key_slots, by_core)

    whole_slots = key_slots.reshape(replicas, capacity, key_width)
    key_slots = key_slots.reshape(halves, low, cores, capacity, key_width)
    stay = lax.dynamic_index_in_dim(key_slots, hi ^ core, 0, keepdims=False)
    come = swap_core(lax.dynamic_index_in_dim(key_slots, hi ^ 1 ^ core, 0, keepdims=False))
    stay, come = jnp.where(core == 0, stay, come), jnp.where(core == 0, come, stay)
    gain_part = gain_part + swap_core(gain_part)
    upper = lax.reduce_precision(gain_part, 8, 7)
    terms = jnp.concatenate([upper, gain_part - upper]).astype(jnp.bfloat16)
    extra = -(-2 * part // (16 * key_width)) * 16
    terms = jnp.pad(terms, (0, extra * key_width - 2 * part)).reshape(1, extra, key_width)
    key_rows = cores * capacity
    routed = jnp.concatenate(
        [
            jnp.stack([stay, come], axis=2).reshape(low, cores * key_rows, key_width),
            jnp.broadcast_to(terms, (low, extra, key_width)),
        ],
        axis=1,
    )
    if low == FEW:
        pieces = [lax.dynamic_index_in_dim(routed, lo ^ s, 0, keepdims=False) for s in range(low)]
        own = pieces[0]
        pieces[PIN], grad_terms = lax.optimization_barrier((pieces[PIN], grad_terms))
        for step in range(low):
            pairs = [
                ((h * low + j) * cores + c, ((h ^ c) * low + (j ^ step)) * cores + c)
                for h in range(halves)
                for j in range(low)
                for c in range(cores)
                if step or c
            ]
            pieces[step] = lax.ppermute(pieces[step], DP, pairs)
        pieces[0] = jnp.where(core == 0, own, pieces[0])
        pieces += [swap_core(piece) for piece in pieces]
        key_out, grad_gain = gather_pieces(pieces, norm_gain, key_rows, factor)
        grad_gain = grad_gain.reshape(width)
    else:
        routed = lax.all_to_all(
            jnp.concatenate(
                [whole_slots, jnp.broadcast_to(terms, (replicas, extra, key_width))], axis=1
            ),
            DP, split_axis=0, concat_axis=0, tiled=True)
        key_out = routed[:, :capacity].reshape(replicas * capacity, key_width)
        gain_sums = routed[:, capacity:].reshape(replicas, extra * key_width)[:, : 2 * part]
        gain_sums = gain_sums.astype(jnp.float32).reshape(halves, low, cores, 2, part)
        gain_sums = jnp.sum(gain_sums[:, :, 0], axis=(0, 2))
        grad_gain = gain_sums.reshape(width) * factor / norm_gain
    return (key_out[None], sum_terms(grad_terms, factor), grad_gain)


def solution(mesh):
    replicas, tensor = mesh.shape["dp"], mesh.shape["tensor"]
    split = Mesh(
        mesh.devices.reshape(2, replicas // 4, 2, tensor), ("hi", "lo", "core", "tensor")
    )
    return jax.shard_map(
        on_device,
        mesh=split,
        in_specs=(
            P(DP, "tensor"),
            P("tensor"),
            P(DP, "tensor"),
            P(DP, None, None),
            P(DP),
            P(DP),
        ),
        out_specs=(P(DP, None, None), P(DP, "tensor"), P("tensor")),
        check_vma=False,
    )
```
